128 devices in a mesh: section: 4 (over y), expert: 32 (over x, z, core).
Axes of the slice: x: 4, y: 4, z: 4, core: 2. Of those that a mesh axis runs over, the one named last changes fastest.
Arguments:
- saved_inputs: bfloat16 [4, 2, 2048, 4096], P('section', None, 'expert'), may hold values from -6 to 6
- arriving: bfloat16 [4, 2048, 4096], P('section', 'expert'), may hold values from -1.5 to 1.5
- last_grad: bfloat16 [2048, 4096], P('expert'), may hold values from -1.5 to 1.5
- expert_ids: int32 [4, 2, 2048, 3], P('section', None, 'expert'), may hold values from 0 to 15, all different within a row; in each aligned block of 64 rows (0 to 63, 64 to 127, ..., all dimensions but the last counted through in order) at most 14 rows name the same one
- combine: bfloat16 [4, 2, 2048, 3], P('section', None, 'expert'), may hold values from 0.099609375 to 1
- w_gate: bfloat16 [4, 32, 4096, 384], P('section', 'expert'), may hold values from -0.09375 to 0.09375
- w_up: bfloat16 [4, 32, 4096, 384], P('section', 'expert'), may hold values from -0.09375 to 0.09375
- w_down: bfloat16 [4, 32, 384, 4096], P('section', 'expert'), may hold values from -0.21875 to 0.21875
Outputs:
- first_grads: bfloat16 [4, 2048, 4096], P('section', 'expert')
- second_grads: bfloat16 [4, 2048, 4096], P('section', 'expert')
- grad_gate: bfloat16 [4, 32, 4096, 384], P('section', 'expert')
- grad_up: bfloat16 [4, 32, 4096, 384], P('section', 'expert')
- grad_down: bfloat16 [4, 32, 384, 4096], P('section', 'expert')
The draws below stay inside these ranges and needn't reach their ends.
Inputs may be any that keep to these rules, and one draw needn't show every extreme that they name: `expert_ids`: each token names 3 different experts. In every aligned block of 64 tokens (the tokens of one device in one section and micro-batch) no expert is named by more than 14 tokens, and in some blocks one expert is named by exactly 14.
All inputs are finite; a program needn't handle non-finite values.
Results may differ from the reference program's by a relative error of at most 0.0085.
Values may be sent and summed in bfloat16 or wider, within the bound.
A program may use at most 192 MiB of HBM per device.

```python
import math
import jax
import jax.numpy as jnp
import numpy as np
from jax import lax

D = 4096
FF = 768
HALVES = 2
TOK_DEV = 64
MICRO = 2
SECTIONS = 4
EXPERTS = 16
SHARDS = 32
FF_DEV = 384
TOP = 3
TOKENS = 2048
CAP = 14


def block_scale(stream_key, dims, cuts, least, high):
    loudness, own = 1.0, jax.random.fold_in(stream_key, 6)
    for position, blocks in cuts:
        heights = jnp.exp(jax.random.uniform(jax.random.fold_in(own, position), (blocks,), jnp.float32, least / len(cuts), high / len(cuts)))
        loudness = loudness * jnp.repeat(heights, dims[position] // blocks).reshape([-1 if axis == position else 1 for axis in range(len(dims))])
    return loudness


def assign_block(stream_key, own, number, rows, count, top, most, lean):
    order = jax.random.permutation(stream_key, count)
    crowded, ordinary = shares(count, rows * top, most, lean, True), shares(count, rows * top, most, lean, False)
    places = jnp.arange(count)

    def named(lengths, offset_by):
        used = int((lengths > 0).sum())
        fixed = max(1, used // 4)
        moved = fixed + (places - fixed + offset_by * (used - fixed)) % max(1, count - fixed)
        return jnp.zeros((count,), jnp.int32).at[order[jnp.where(places < fixed, places, moved)]].set(jnp.asarray(lengths, jnp.int32))

    lengths = jnp.where(number % 4 == 0, named(crowded, number // 4), named(ordinary, number - number // 4 - 1))
    mixed = jax.random.permutation(jax.random.fold_in(own, 3), count)
    donor, sink = mixed[0:count // 2 * 2:2], mixed[1:count // 2 * 2:2]
    margin = jnp.minimum(lengths[donor] - 1, most - lengths[sink]) // 2
    margin = jnp.where((donor == order[0]) | (sink == order[0]) | (lengths[sink] == 0), 0, jnp.maximum(margin, 0))
    moved = jax.random.randint(jax.random.fold_in(own, 4), (count // 2,), 0, 1 << 20) % (margin + 1)
    lengths = lengths.at[donor].add(-moved).at[sink].add(moved)
    members = jnp.searchsorted(jnp.cumsum(lengths), jnp.arange(rows * top), side="right").astype(jnp.int32)
    grid = members.reshape(top, rows).T
    grid = grid[jax.random.permutation(jax.random.fold_in(own, 1), rows)]
    offset_by = jax.random.randint(jax.random.fold_in(own, 2), (rows, 1), 0, top)
    return jnp.take_along_axis(grid, (jnp.arange(top)[None, :] + offset_by) % top, axis=1)


def shares(amount, total, limit, skew, full):
    loads = [(1 << 20) // math.isqrt(standing ** skew) + 1 for standing in range(1, amount + 1)]
    largest = limit if full else min(limit, max(-(-total // amount), total * loads[0] // sum(loads)))
    least = 1 if total - largest >= amount - 1 else 0
    holding, rest = [largest] + [least] * (amount - 1), total - largest - least * (amount - 1)
    while rest > 0:
        free = [i for i in range(1, amount) if holding[i] < largest] or [i for i in range(1, amount) if holding[i] < limit]
        mass, left = sum([loads[i] for i in free]), rest
        for i in free:
            extra = min(limit - holding[i], max(1, left * loads[i] // mass), rest)
            holding[i] = holding[i] + extra
            rest = rest - extra
    return np.array(holding)


def centred(own_key, extent, scale, bound, shards=(), kind=jnp.bfloat16):
    values = scale * jax.random.normal(own_key, extent, jnp.float32)
    if shards:
        values = values * block_scale(own_key, extent, shards, -0.22, 0.18)
    return jnp.clip(values, -bound, bound).astype(kind)


def setup_inputs(seed: int = 0) -> dict:
    arg_keys = jax.random.split(jax.random.key(seed), 9)
    saved_inputs = centred(arg_keys[0], (SECTIONS, MICRO, TOKENS, D), 1.0, 6.0, ((0, 4), (2, 32)))
    arriving = centred(arg_keys[1], (SECTIONS, TOKENS, D), 0.25, 1.5, ((0, 4), (1, 32)))
    last_grad = centred(arg_keys[2], (TOKENS, D), 0.25, 1.5, ((0, 32),))
    expert_ids_keys = jax.random.split(jax.random.fold_in(arg_keys[3], 1), SECTIONS * MICRO * TOKENS // TOK_DEV)
    expert_ids_turns = jax.random.permutation(jax.random.fold_in(arg_keys[3], 3), SECTIONS * MICRO * TOKENS // TOK_DEV)
    expert_ids = jax.vmap(lambda own, number: assign_block(jax.random.fold_in(arg_keys[3], 2), own, number, TOK_DEV, EXPERTS, TOP, CAP, 1))(expert_ids_keys, expert_ids_turns).reshape((SECTIONS, MICRO, TOKENS, TOP))
    combine = jnp.clip(0.099609375 + 0.9003906 * jax.random.uniform(arg_keys[4], (SECTIONS, MICRO, TOKENS, TOP), jnp.float32) ** block_scale(arg_keys[4], (SECTIONS, MICRO, TOKENS, TOP), ((0, 4), (2, 32)), -0.2, 0.2), 0.099609375, 1.0).astype(jnp.bfloat16)
    w_gate = centred(arg_keys[5], (SECTIONS, SHARDS, D, FF_DEV), D ** -0.5, 0.09375, ((0, 4), (1, 32)))
    w_up = centred(arg_keys[6], (SECTIONS, SHARDS, D, FF_DEV), D ** -0.5, 0.09375, ((0, 4), (1, 32)))
    w_down = centred(arg_keys[7], (SECTIONS, SHARDS, FF_DEV, D), FF ** -0.5, 0.21875, ((0, 4), (1, 32)))
    return {"saved_inputs": saved_inputs, "arriving": arriving, "last_grad": last_grad, "expert_ids": expert_ids, "combine": combine, "w_gate": w_gate, "w_up": w_up, "w_down": w_down}


def rows_backward(x_rows, weighted, gate_w, up_w, down_w):
    gate_pre = jnp.dot(x_rows, gate_w, preferred_element_type=jnp.float32)
    up_pre = jnp.dot(x_rows, up_w, preferred_element_type=jnp.float32)
    gate_sigmoid = jax.nn.sigmoid(gate_pre)
    active = gate_pre * gate_sigmoid
    hidden = (active * up_pre).astype(jnp.bfloat16)
    contract = (((1,), (1,)), ((), ()))
    hidden_grad = lax.dot_general(weighted, down_w, contract, preferred_element_type=jnp.float32)
    gate_rows = (hidden_grad * up_pre * gate_sigmoid * (1.0 + gate_pre * (1.0 - gate_sigmoid))).astype(jnp.bfloat16)
    up_rows = (hidden_grad * active).astype(jnp.bfloat16)
    partial_value = lax.dot_general(gate_rows, gate_w, contract, preferred_element_type=jnp.float32)
    partial_value = partial_value + lax.dot_general(up_rows, up_w, contract, preferred_element_type=jnp.float32)
    return partial_value, hidden, gate_rows, up_rows


def weight_terms(pieces):
    x_rows, weighted, hidden, gate_rows, up_rows = pieces
    across = (((0,), (0,)), ((), ()))
    return (lax.dot_general(x_rows, gate_rows, across, preferred_element_type=jnp.float32),
            lax.dot_general(x_rows, up_rows, across, preferred_element_type=jnp.float32),
            lax.dot_general(hidden, weighted, across, preferred_element_type=jnp.float32))


def slot_numbers(route_ids):
    block_count = TOKENS // TOK_DEV
    flat_ids = route_ids.reshape(block_count, TOK_DEV * TOP)
    onehot = (flat_ids[:, :, None] == jnp.arange(EXPERTS, dtype=jnp.int32)[None, None, :]).astype(jnp.int32)
    before = (jnp.cumsum(onehot, axis=1) - onehot).astype(jnp.int32)
    return jnp.sum(before * onehot, axis=2).astype(jnp.int32).reshape(TOKENS, TOP)


def section_backward(inputs, grads_in, route_ids, weights, w_gate, w_up, w_down):
    block_count = TOKENS // TOK_DEV
    slots = slot_numbers(route_ids)
    source_block = jnp.broadcast_to((jnp.arange(TOKENS, dtype=jnp.int32) // TOK_DEV)[:, None], (TOKENS, TOP)).astype(jnp.int32)
    weighted_all = (weights.astype(jnp.float32)[:, :, None] * grads_in.astype(jnp.float32)[:, None, :]).astype(jnp.bfloat16)
    inputs_all = jnp.broadcast_to(inputs[:, None, :], (TOKENS, TOP, D))
    x_buf = jnp.zeros((EXPERTS, block_count, CAP, D), jnp.bfloat16).at[route_ids, source_block, slots].set(inputs_all)
    w_buf = jnp.zeros((EXPERTS, block_count, CAP, D), jnp.bfloat16).at[route_ids, source_block, slots].set(weighted_all)

    def one_shard(items):
        shard_index, gate_w, up_w, down_w = items
        expert_index = shard_index // HALVES
        x_rows = x_buf[expert_index].reshape(block_count * CAP, D)
        weighted = w_buf[expert_index].reshape(block_count * CAP, D)
        partial_value, hidden, gate_rows, up_rows = rows_backward(x_rows, weighted, gate_w, up_w, down_w)
        grads = weight_terms((x_rows, weighted, hidden, gate_rows, up_rows))
        return partial_value.reshape(block_count, CAP, D), grads[0], grads[1], grads[2]

    partials, grad_g, grad_u, grad_d = lax.map(one_shard, (jnp.arange(SHARDS, dtype=jnp.int32), w_gate, w_up, w_down))
    expert_partial = jnp.sum(partials.reshape(EXPERTS, HALVES, block_count, CAP, D), axis=1).astype(jnp.bfloat16)
    picked = expert_partial[route_ids, source_block, slots]
    expert_sum = jnp.sum(picked.astype(jnp.float32), axis=1)
    result = (grads_in.astype(jnp.float32) + expert_sum).astype(jnp.bfloat16)
    return result, grad_g, grad_u, grad_d


def reference(saved_inputs, arriving, last_grad, expert_ids, combine, w_gate, w_up, w_down):
    first_list = [None] * SECTIONS
    second_list = [None] * SECTIONS
    gate_list = [None] * SECTIONS
    up_list = [None] * SECTIONS
    down_list = [None] * SECTIONS
    for section in range(SECTIONS - 1, -1, -1):
        first_grad, g_one, u_one, d_one = section_backward(saved_inputs[section, 0], arriving[section], expert_ids[section, 0], combine[section, 0], w_gate[section], w_up[section], w_down[section])
        if section == SECTIONS - 1:
            incoming = last_grad
        else:
            incoming = first_list[section + 1]
        second_grad, g_two, u_two, d_two = section_backward(saved_inputs[section, 1], incoming, expert_ids[section, 1], combine[section, 1], w_gate[section], w_up[section], w_down[section])
        first_list[section] = first_grad
        second_list[section] = second_grad
        gate_list[section] = (g_one + g_two).astype(jnp.bfloat16)
        up_list[section] = (u_one + u_two).astype(jnp.bfloat16)
        down_list[section] = (d_one + d_two).astype(jnp.bfloat16)
    return (jnp.stack(first_list), jnp.stack(second_list), jnp.stack(gate_list), jnp.stack(up_list), jnp.stack(down_list))
```

```python
import jax
import jax.numpy as jnp
from jax import lax
from jax.experimental import pallas as pl
from jax.experimental.pallas import tpu as pltpu
from jax.sharding import PartitionSpec as P

MESH = pl.DeviceIdType.MESH
F32 = jnp.float32
BF16 = jnp.bfloat16

RING = 4
PEERS = RING * RING
ROWS = 16
CAP = 14
GROUP = 512
FULL = 7
WIDE = FULL * GROUP
D = 4096
TOK = 64
FF = 384
ALL = PEERS * ROWS

ORDER = tuple(
    (dx % RING) * RING + dz % RING
    for dx, dz in (
        (2, 2), (1, 0), (-1, 0), (2, 1), (0, -1), (1, 2), (0, 1), (2, -1),
        (1, 1), (-1, 2), (-1, -1), (2, 0), (1, -1), (0, 2), (-1, 1),
    )
)

ACROSS = (((1,), (1,)), ((), ()))
DOWN = (((0,), (0,)), ((), ()))


def mm(a, b):
    return jnp.dot(a, b, preferred_element_type=F32)


def mm_t(a, b):
    return lax.dot_general(a, b, ACROSS, preferred_element_type=F32)


def iota(shape, axis):
    return lax.broadcasted_iota(jnp.int32, shape, axis)


def spread(group, transposed):
    to, come = iota((ALL, ALL), int(transposed)), iota((ALL, ALL), int(not transposed))
    slot = to % ROWS
    late = (slot >= 7).astype(jnp.int32)
    hit = jnp.logical_and(come == to - slot + CAP + late, slot - 7 * late == group)
    return hit.astype(F32).astype(BF16)


def cols(group):
    return pl.ds(pl.multiple_of(group * GROUP, GROUP), GROUP)


def kernel(
    x_ref, dy_ref, last_ref, ids_ref, comb_ref, wg_ref, wu_ref, wd_ref,
    first_ref, second_ref, gg_ref, gu_ref, gd_ref,
    wgu, wd, xs, ws, gs, hs, g_far, h_far, send, back, got, dy_next,
    pre, hg, key, key_t, comb_t, h_t, stage_gu, stage_d,
    ssem, rsem, wsem, pair_send, pair_recv, y_send, y_recv, osem,
):
    section = lax.axis_index("section")
    place = lax.axis_index("expert")
    at_x, at_z, core = place // (2 * RING), (place // 2) % RING, place % 2

    def chip(slot, sign):
        dx, dz = slot // RING, slot % RING
        if sign < 0:
            dx, dz = (RING - dx) % RING, (RING - dz) % RING
        where = ((at_x + dx) % RING) * RING + (at_z + dz) % RING
        return (section, where * 2 + core)

    partner = (section, place + 1 - 2 * core)
    before = ((section + RING - 1) % RING, place)
    after = ((section + 1) % RING, place)

    barrier = pltpu.get_barrier_semaphore()
    for slot in range(1, PEERS):
        pl.semaphore_signal(barrier, inc=1, device_id=chip(slot, 1), device_id_type=MESH)
    pl.semaphore_signal(barrier, inc=1, device_id=partner, device_id_type=MESH)
    pl.semaphore_signal(barrier, inc=1, device_id=after, device_id_type=MESH)

    own = [
        pltpu.make_async_copy(wg_ref.at[0, 0], wgu.at[0, :, pl.ds(0, FF)], wsem.at[0]),
        pltpu.make_async_copy(wu_ref.at[0, 0], wgu.at[0, :, pl.ds(FF, FF)], wsem.at[1]),
        pltpu.make_async_copy(wd_ref.at[0, 0], wd.at[pl.ds(0, FF), :], wsem.at[2]),
    ]
    for copy in own:
        copy.start()

    def tables(m):
        ids = ids_ref[0, m]
        ids = jnp.concatenate([ids, ids], axis=0)
        weights = comb_ref[0, m].astype(F32)
        weights = jnp.concatenate([weights, weights], axis=0)
        lane = iota((2 * TOK, ALL), 1)
        row = iota((2 * TOK, ALL), 0)
        slot, c = lane // ROWS, lane % ROWS
        expert = ((at_x + slot // RING) % RING) * RING + (at_z + slot % RING) % RING
        named = jnp.zeros((2 * TOK, ALL), F32)
        combined = jnp.zeros((2 * TOK, ALL), F32)
        for k in range(3):
            hit = ids[:, k : k + 1] == expert
            named = jnp.where(hit, 1.0, named)
            combined = jnp.where(hit, weights[:, k : k + 1], combined)
        r2, c2 = iota((2 * TOK, 2 * TOK), 0), iota((2 * TOK, 2 * TOK), 1)
        earlier = (c2 < r2 % TOK).astype(F32).astype(BF16)
        rank = mm(earlier, named.astype(BF16))
        top = row < TOK
        base = jnp.where(top, c, 7 * (c - CAP)).astype(F32)
        fits = jnp.logical_and(named > 0.5, top == (c < CAP))
        value = jnp.where(fits, rank - base, -100.0)
        key[m] = value
        key_t[m] = value.T
        comb_t[m] = combined.T

    def payload(m, source, scaled, buf, rows_ref, base):
        def body(g, carry):
            data = jnp.concatenate([source[:, cols(g)], source[:, pl.ds(WIDE, GROUP)]], axis=0)
            lane = iota((ALL, 2 * TOK), 1)
            wanted = jnp.where(lane < TOK, 0, g).astype(F32)
            table = jnp.where(key_t[m] == wanted, comb_t[m] if scaled else 1.0, 0.0)
            value = mm(table.astype(BF16), data).astype(BF16)
            send[buf, :, cols(g)] = value
            rows_ref[pl.ds(base, ROWS), cols(g)] = value[:ROWS]
            return carry

        lax.fori_loop(0, FULL, body, 0)

    def dispatch(phase, buf, rows_ref, base, slots):
        for slot in slots:
            pltpu.make_async_remote_copy(
                src_ref=send.at[buf, pl.ds(slot * ROWS, ROWS), :],
                dst_ref=rows_ref.at[pl.ds(base + slot * ROWS, ROWS), pl.ds(0, WIDE)],
                send_sem=ssem.at[phase],
                recv_sem=rsem.at[phase],
                device_id=chip(slot, 1),
                device_id_type=MESH,
            ).start()

    def sent(phase, ref):
        part = ref.at[pl.ds(ROWS, ALL - ROWS), :]
        pltpu.make_async_copy(part, part, ssem.at[phase]).wait()

    def arrived(phase, ref, base):
        part = ref.at[pl.ds(base + ROWS, ALL - ROWS), pl.ds(0, WIDE)]
        pltpu.make_async_copy(part, part, rsem.at[phase]).wait()

    def unfold(ref, base):
        total = jnp.zeros((ALL, GROUP), F32)
        for g in range(FULL):
            total = total + mm(
                spread(g, False), ref[pl.ds(base, ALL), pl.ds(g * GROUP, GROUP)]
            )
        ref[pl.ds(base, ALL), pl.ds(WIDE, GROUP)] = total.astype(BF16)

    def to_partner(n, src, dst):
        return pltpu.make_async_remote_copy(
            src_ref=src, dst_ref=dst, send_sem=pair_send.at[n], recv_sem=pair_recv.at[n],
            device_id=partner, device_id_type=MESH,
        )

    def rows_of(part):
        return pl.ds(part * ALL, ALL)

    def forward(m):
        base = 2 * m * ALL

        def body(n, carry):
            half, tile = n // 3, pl.ds(pl.multiple_of((n % 3) * 256, 256), 256)
            pre[half, :, tile] = mm(xs[pl.ds(base, ALL), :], wgu[half, :, tile])
            return carry

        lax.fori_loop(0, 6, body, 0)

    def hidden_terms(m):
        base = 2 * m * ALL

        def body(n, carry):
            tile = pl.ds(pl.multiple_of(n * 256, 256), 256)
            hg[:, tile] = mm_t(ws[pl.ds(base, ALL), :], wd[tile, :])
            return carry

        lax.fori_loop(0, 3, body, 0)
        real = iota((ALL, FF), 0) % ROWS < CAP
        for half in range(2):
            gate, up = pre[half, :, :FF], pre[half, :, FF:]
            grad = hg[:, half * FF : (half + 1) * FF]
            sig = jax.nn.sigmoid(gate)
            active = gate * sig
            hidden = jnp.where(real, active * up, 0.0).astype(BF16)
            gate_rows = grad * up * sig * (1.0 + gate * (1.0 - sig))
            gate_rows = jnp.where(real, gate_rows, 0.0).astype(BF16)
            up_rows = jnp.where(real, grad * active, 0.0).astype(BF16)
            if half == 0:
                gs[pl.ds(base, ALL), :FF] = gate_rows
                gs[pl.ds(base, ALL), FF:] = up_rows
                hs[pl.ds(base, ALL), :] = hidden
            else:
                g_far[m, :, :FF] = gate_rows
                g_far[m, :, FF:] = up_rows
                h_far[m] = hidden

    def partial(m, g):
        base = 2 * m * ALL
        near = mm_t(gs[pl.ds(base, ALL), :], wgu[0, cols(g), :])
        return near + mm_t(g_far[m], wgu[1, cols(g), :])

    def partials(m):
        folded = partial(m, FULL).astype(BF16)

        def body(g, carry):
            value = (partial(m, g) + mm(spread(g, True), folded)).astype(BF16)
            back[:, cols(g)] = value
            got[pl.ds(0, ROWS), cols(g)] = value[:ROWS]
            return carry

        lax.fori_loop(0, FULL, body, 0)

    def give_back(phase):
        for slot in ORDER:
            pltpu.make_async_remote_copy(
                src_ref=back.at[pl.ds(slot * ROWS, ROWS), :],
                dst_ref=got.at[pl.ds(slot * ROWS, ROWS), :],
                send_sem=ssem.at[phase],
                recv_sem=rsem.at[phase],
                device_id=chip(slot, -1),
                device_id_type=MESH,
            ).start()

    def combine(m, grads, out):
        picked = jnp.where(key[m, :TOK] == 0.0, 1.0, 0.0).astype(BF16)

        def body(g, total):
            block = got[:, cols(g)]
            out[0, :, cols(g)] = (grads[:, cols(g)].astype(F32) + mm(picked, block)).astype(BF16)
            folded = jnp.where(key[m, TOK:] == g.astype(F32), 1.0, 0.0).astype(BF16)
            return total + mm(folded, block)

        total = lax.fori_loop(0, FULL, body, jnp.zeros((TOK, GROUP), F32))
        tail = pl.ds(WIDE, GROUP)
        out[0, :, tail] = (grads[:, tail].astype(F32) + total).astype(BF16)

    tables(0)
    payload(0, x_ref.at[0, 0], False, 0, xs, 0)
    pl.semaphore_wait(barrier, PEERS + 1)
    dispatch(0, 0, xs, 0, ORDER)
    far = [
        to_partner(0, wg_ref.at[0, 0], wgu.at[1, :, pl.ds(0, FF)]),
        to_partner(1, wu_ref.at[0, 0], wgu.at[1, :, pl.ds(FF, FF)]),
        to_partner(2, wd_ref.at[0, 0], wd.at[pl.ds(FF, FF), :]),
    ]
    for copy in far:
        copy.start()
    payload(0, dy_ref.at[0], True, 1, ws, 0)
    dispatch(1, 1, ws, 0, ORDER)
    tables(1)
    payload(1, x_ref.at[0, 1], False, 2, xs, 2 * ALL)
    dispatch(3, 2, xs, 2 * ALL, ORDER[:5])

    for copy in own:
        copy.wait()
    for copy in far:
        copy.wait()
    arrived(0, xs, 0)
    unfold(xs, 0)
    pair = [to_partner(3, xs.at[rows_of(0), :], xs.at[rows_of(1), :])]
    pair[-1].start()
    forward(0)
    arrived(1, ws, 0)
    unfold(ws, 0)
    pair.append(to_partner(4, ws.at[rows_of(0), :], ws.at[rows_of(1), :]))
    pair[-1].start()
    hidden_terms(0)
    partials(0)
    give_back(2)
    dispatch(3, 2, xs, 2 * ALL, ORDER[5:])
    pair.append(to_partner(5, g_far.at[0], gs.at[rows_of(1), :]))
    pair[-1].start()
    pair.append(to_partner(6, h_far.at[0], hs.at[rows_of(1), :]))
    pair[-1].start()
    sent(0, send.at[0])

    arrived(2, got, 0)
    combine(0, dy_ref.at[0], first_ref)
    relay = pltpu.make_async_remote_copy(
        src_ref=first_ref.at[0], dst_ref=dy_next, send_sem=y_send, recv_sem=y_recv,
        device_id=before, device_id_type=MESH,
    )
    relay.start()
    relay.wait()

    @pl.when(section == RING - 1)
    def _():
        dy_next[...] = last_ref[...]

    payload(1, dy_next, True, 0, ws, 2 * ALL)
    dispatch(4, 0, ws, 2 * ALL, ORDER)
    sent(2, back)
    arrived(3, xs, 2 * ALL)
    unfold(xs, 2 * ALL)
    pair.append(to_partner(7, xs.at[rows_of(2), :], xs.at[rows_of(3), :]))
    pair[-1].start()
    forward(1)
    arrived(4, ws, 2 * ALL)
    unfold(ws, 2 * ALL)
    pair.append(to_partner(8, ws.at[rows_of(2), :], ws.at[rows_of(3), :]))
    pair[-1].start()
    hidden_terms(1)
    pair.append(to_partner(9, g_far.at[1], gs.at[rows_of(3), :]))
    pair[-1].start()
    pair.append(to_partner(10, h_far.at[1], hs.at[rows_of(3), :]))
    pair[-1].start()
    partials(1)
    give_back(5)

    for copy in pair:
        copy.wait()
    h_t[...] = hs[...].astype(F32).T.astype(BF16)

    def stores(d):
        slot = d % 2
        rows = cols(d)
        return [
            pltpu.make_async_copy(
                stage_gu.at[slot, :, pl.ds(0, FF)], gg_ref.at[0, 0, rows, :], osem.at[slot, 0]
            ),
            pltpu.make_async_copy(
                stage_gu.at[slot, :, pl.ds(FF, FF)], gu_ref.at[0, 0, rows, :], osem.at[slot, 1]
            ),
            pltpu.make_async_copy(stage_d.at[slot], gd_ref.at[0, 0, :, rows], osem.at[slot, 2]),
        ]

    def weight_body(d, carry):
        @pl.when(d >= 2)
        def _():
            for copy in stores(d - 2):
                copy.wait()

        slot = d % 2
        value = lax.dot_general(xs[:, cols(d)], gs[...], DOWN, preferred_element_type=F32)
        stage_gu[slot] = value.astype(BF16)
        stage_d[slot] = mm(h_t[...], ws[:, cols(d)]).astype(BF16)
        for copy in stores(d):
            copy.start()
        return carry

    lax.fori_loop(0, D // GROUP, weight_body, 0)

    arrived(5, got, 0)
    combine(1, dy_next, second_ref)
    for d in range(D // GROUP - 2, D // GROUP):
        for copy in stores(d):
            copy.wait()
    sent(1, send.at[1])
    sent(3, send.at[2])
    sent(4, send.at[0])
    sent(5, back)


def local(saved_inputs, arriving, last_grad, expert_ids, combine, w_gate, w_up, w_down):
    vmem = pl.BlockSpec(memory_space=pltpu.VMEM)
    hbm = pl.BlockSpec(memory_space=pl.ANY)
    grads = jax.ShapeDtypeStruct(arriving.shape, BF16)
    dma = pltpu.SemaphoreType.DMA
    return pl.pallas_call(
        kernel,
        out_shape=(
            grads,
            grads,
            jax.ShapeDtypeStruct(w_gate.shape, BF16),
            jax.ShapeDtypeStruct(w_up.shape, BF16),
            jax.ShapeDtypeStruct(w_down.shape, BF16),
        ),
        in_specs=[vmem] * 5 + [hbm] * 3,
        out_specs=(vmem, vmem, hbm, hbm, hbm),
        scratch_shapes=[
            pltpu.VMEM((2, D, 2 * FF), BF16),
            pltpu.VMEM((2 * FF, D), BF16),
            pltpu.VMEM((4 * ALL, D), BF16),
            pltpu.VMEM((4 * ALL, D), BF16),
            pltpu.VMEM((4 * ALL, 2 * FF), BF16),
            pltpu.VMEM((4 * ALL, FF), BF16),
            pltpu.VMEM((2, ALL, 2 * FF), BF16),
            pltpu.VMEM((2, ALL, FF), BF16),
            pltpu.VMEM((3, ALL, WIDE), BF16),
            pltpu.VMEM((ALL, WIDE), BF16),
            pltpu.VMEM((ALL, WIDE), BF16),
            pltpu.VMEM((TOK, D), BF16),
            pltpu.VMEM((2, ALL, 2 * FF), F32),
            pltpu.VMEM((ALL, 2 * FF), F32),
            pltpu.VMEM((2, 2 * TOK, ALL), F32),
            pltpu.VMEM((2, ALL, 2 * TOK), F32),
            pltpu.VMEM((2, ALL, 2 * TOK), F32),
            pltpu.VMEM((FF, 4 * ALL), BF16),
            pltpu.VMEM((2, GROUP, 2 * FF), BF16),
            pltpu.VMEM((2, FF, GROUP), BF16),
            dma((6,)),
            dma((6,)),
            dma((3,)),
            dma((11,)),
            dma((11,)),
            dma,
            dma,
            dma((2, 3)),
        ],
        compiler_params=pltpu.CompilerParams(
            collective_id=0, has_side_effects=True, vmem_limit_bytes=63 << 20
        ),
        name="relay_backward",
    )(saved_inputs, arriving, last_grad, expert_ids, combine, w_gate, w_up, w_down)


def solution(mesh):
    return jax.shard_map(
        local,
        mesh=mesh,
        in_specs=(
            P("section", None, "expert", None),
            P("section", "expert", None),
            P("expert", None),
            P("section", None, "expert", None),
            P("section", None, "expert", None),
            P("section", "expert", None, None),
            P("section", "expert", None, None),
            P("section", "expert", None, None),
        ),
        out_specs=(
            P("section", "expert", None),
            P("section", "expert", None),
            P("section", "expert", None, None),
            P("section", "expert", None, None),
            P("section", "expert", None, None),
        ),
        check_vma=False,
    )
```

```python
import jax
import jax.numpy as jnp
from jax import lax
from jax.experimental import pallas as pl
from jax.experimental.pallas import tpu as pltpu
from jax.sharding import PartitionSpec as P

MESH = pl.DeviceIdType.MESH
F32 = jnp.float32
BF16 = jnp.bfloat16

RING = 4
PEERS = RING * RING
ROWS = 16
CAP = 14
GROUP = 512
FULL = 7
WIDE = FULL * GROUP
D = 4096
TOK = 64
FF = 384
ALL = PEERS * ROWS

STEPS = (
    (0, 0), (2, 2), (1, 0), (-1, 2), (0, 1), (2, 1), (0, -1), (2, -1),
    (1, 2), (-1, 0), (1, 1), (0, 2), (-1, -1), (2, 0), (1, -1), (-1, 1),
)
EARLY, LATE = range(1, 8), range(8, 16)
HALF = ALL // 2

ACROSS = (((1,), (1,)), ((), ()))
DOWN = (((0,), (0,)), ((), ()))


def mm(a, b):
    return jnp.dot(a, b, preferred_element_type=F32)


def mm_t(a, b):
    return lax.dot_general(a, b, ACROSS, preferred_element_type=F32)


def iota(shape, axis):
    return lax.broadcasted_iota(jnp.int32, shape, axis)


def spread(group, transposed, count):
    to, come = iota((count, count), int(transposed)), iota((count, count), int(not transposed))
    slot = to % ROWS
    late = (slot >= 7).astype(jnp.int32)
    hit = jnp.logical_and(come == to - slot + CAP + late, slot - 7 * late == group)
    return hit.astype(F32).astype(BF16)


def cols(group):
    return pl.ds(pl.multiple_of(group * GROUP, GROUP), GROUP)


def kernel(
    x_ref, dy_ref, last_ref, ids_ref, comb_ref, wg_ref, wu_ref, wd_ref,
    first_ref, second_ref, gg_ref, gu_ref, gd_ref,
    wgu, wd, xs, ws, gs, hs, g_far, h_far, send, back, got, dy_next,
    pre, hg, key, key_t, comb_t, h_t, stage_gu, stage_d,
    ssem, rsem, wsem, pair_send, pair_recv, y_send, y_recv, osem,
):
    section = lax.axis_index("section")
    place = lax.axis_index("expert")
    at_x, at_z, core = place // (2 * RING), (place // 2) % RING, place % 2

    def expert_at(slot, sign):
        dx, dz = (sign * step % RING for step in STEPS[slot])
        return ((at_x + dx) % RING) * RING + (at_z + dz) % RING

    def chip(slot, sign):
        return (section, expert_at(slot, sign) * 2 + core)

    partner = (section, place + 1 - 2 * core)
    before = ((section + RING - 1) % RING, place)
    after = ((section + 1) % RING, place)

    barrier = pltpu.get_barrier_semaphore()
    for slot in range(1, PEERS):
        pl.semaphore_signal(barrier, inc=1, device_id=chip(slot, 1), device_id_type=MESH)
    pl.semaphore_signal(barrier, inc=1, device_id=partner, device_id_type=MESH)
    pl.semaphore_signal(barrier, inc=1, device_id=after, device_id_type=MESH)

    own = [
        pltpu.make_async_copy(wg_ref.at[0, 0], wgu.at[0, :, pl.ds(0, FF)], wsem.at[0]),
        pltpu.make_async_copy(wu_ref.at[0, 0], wgu.at[0, :, pl.ds(FF, FF)], wsem.at[1]),
        pltpu.make_async_copy(wd_ref.at[0, 0], wd.at[pl.ds(0, FF), :], wsem.at[2]),
    ]
    for copy in own:
        copy.start()

    def tables(m):
        shape = (ALL, 2 * TOK)
        row, lane = iota(shape, 0), iota(shape, 1)
        c = row % ROWS
        expert = jnp.concatenate(
            [jnp.full((ROWS, 2 * TOK), expert_at(slot, 1), jnp.int32) for slot in range(PEERS)], axis=0
        )
        named = jnp.zeros(shape, F32)
        combined = jnp.zeros(shape, F32)
        for k in range(3):
            ids = ids_ref[0, k, m : m + 1, :]
            weights = comb_ref[0, k, m : m + 1, :].astype(F32)
            hit = jnp.concatenate([ids, ids], axis=1) == expert
            named = jnp.where(hit, 1.0, named)
            combined = jnp.where(hit, jnp.concatenate([weights, weights], axis=1), combined)
        r2, c2 = iota((2 * TOK, 2 * TOK), 0), iota((2 * TOK, 2 * TOK), 1)
        earlier = (r2 < c2 % TOK).astype(F32).astype(BF16)
        rank = mm(named.astype(BF16), earlier)
        top = lane < TOK
        base = jnp.where(top, c, 7 * (c - CAP)).astype(F32)
        fits = jnp.logical_and(named > 0.5, top == (c < CAP))
        value = jnp.where(fits, rank - base, -100.0)
        key_t[m] = value
        key[m] = value.T
        comb_t[m] = combined

    def payload(m, source, scaled, buf, rows_ref, base):
        def body(g, carry):
            data = jnp.concatenate([source[:, cols(g)], source[:, pl.ds(WIDE, GROUP)]], axis=0)
            lane = iota((ALL, 2 * TOK), 1)
            wanted = jnp.where(lane < TOK, 0, g).astype(F32)
            table = jnp.where(key_t[m] == wanted, comb_t[m] if scaled else 1.0, 0.0)
            value = mm(table.astype(BF16), data).astype(BF16)
            send[buf, :, cols(g)] = value
            rows_ref[pl.ds(base, ROWS), cols(g)] = value[:ROWS]
            return carry

        lax.fori_loop(0, FULL, body, 0)

    def dispatch(phase, buf, rows_ref, base, slots):
        for slot in slots:
            pltpu.make_async_remote_copy(
                src_ref=send.at[buf, pl.ds(slot * ROWS, ROWS), :],
                dst_ref=rows_ref.at[pl.ds(base + slot * ROWS, ROWS), pl.ds(0, WIDE)],
                send_sem=ssem.at[phase],
                recv_sem=rsem.at[phase],
                device_id=chip(slot, 1),
                device_id_type=MESH,
            ).start()

    def sent(phase, ref, lo=ROWS, hi=ALL):
        part = ref.at[pl.ds(lo, hi - lo), :]
        pltpu.make_async_copy(part, part, ssem.at[phase]).wait()

    def arrived(phase, ref, base, lo=ROWS, hi=ALL):
        part = ref.at[pl.ds(base + lo, hi - lo), pl.ds(0, WIDE)]
        pltpu.make_async_copy(part, part, rsem.at[phase]).wait()

    def unfold(ref, base, count):
        total = jnp.zeros((count, GROUP), F32)
        for g in range(FULL):
            total = total + mm(
                spread(g, False, count), ref[pl.ds(base, count), pl.ds(g * GROUP, GROUP)]
            )
        ref[pl.ds(base, count), pl.ds(WIDE, GROUP)] = total.astype(BF16)

    def to_partner(n, src, dst):
        return pltpu.make_async_remote_copy(
            src_ref=src, dst_ref=dst, send_sem=pair_send.at[n], recv_sem=pair_recv.at[n],
            device_id=partner, device_id_type=MESH,
        )

    def rows_of(part):
        return pl.ds(part * ALL, ALL)

    def forward(m):
        base = 2 * m * ALL

        def body(n, carry):
            half, tile = n // 3, pl.ds(pl.multiple_of((n % 3) * 256, 256), 256)
            pre[half, :, tile] = mm(xs[pl.ds(base, ALL), :], wgu[half, :, tile])
            return carry

        lax.fori_loop(0, 6, body, 0)

    def hidden_terms(m, lo, count):
        base = 2 * m * ALL + lo

        def body(n, carry):
            tile = pl.ds(pl.multiple_of(n * 256, 256), 256)
            hg[pl.ds(lo, count), tile] = mm_t(ws[pl.ds(base, count), :], wd[tile, :])
            return carry

        lax.fori_loop(0, 3, body, 0)
        real = iota((count, FF), 0) % ROWS < CAP
        part = pl.ds(lo, count)
        for half in range(2):
            gate, up = pre[half, part, :FF], pre[half, part, FF:]
            grad = hg[part, half * FF : (half + 1) * FF]
            sig = jax.nn.sigmoid(gate)
            active = gate * sig
            hidden = jnp.where(real, active * up, 0.0).astype(BF16)
            gate_rows = grad * up * sig * (1.0 + gate * (1.0 - sig))
            gate_rows = jnp.where(real, gate_rows, 0.0).astype(BF16)
            up_rows = jnp.where(real, grad * active, 0.0).astype(BF16)
            if half == 0:
                gs[pl.ds(base, count), :FF] = gate_rows
                gs[pl.ds(base, count), FF:] = up_rows
                hs[pl.ds(base, count), :] = hidden
            else:
                g_far[m, part, :FF] = gate_rows
                g_far[m, part, FF:] = up_rows
                h_far[m, part, :] = hidden

    def partials(m, lo, count):
        def partial(g):
            near = mm_t(gs[pl.ds(2 * m * ALL + lo, count), :], wgu[0, cols(g), :])
            return near + mm_t(g_far[m, pl.ds(lo, count), :], wgu[1, cols(g), :])

        folded = partial(FULL).astype(BF16)

        def body(g, carry):
            value = (partial(g) + mm(spread(g, True, count), folded)).astype(BF16)
            back[pl.ds(lo, count), cols(g)] = value
            if lo == 0:
                got[pl.ds(0, ROWS), cols(g)] = value[:ROWS]
            return carry

        lax.fori_loop(0, FULL, body, 0)

    def give_back(phase, slots):
        for slot in slots:
            pltpu.make_async_remote_copy(
                src_ref=back.at[pl.ds(slot * ROWS, ROWS), :],
                dst_ref=got.at[pl.ds(slot * ROWS, ROWS), :],
                send_sem=ssem.at[phase],
                recv_sem=rsem.at[phase],
                device_id=chip(slot, -1),
                device_id_type=MESH,
            ).start()

    def combine(m, grads, out):
        picked = jnp.where(key[m, :TOK] == 0.0, 1.0, 0.0).astype(BF16)

        def body(g, total):
            block = got[:, cols(g)]
            out[0, :, cols(g)] = (grads[:, cols(g)].astype(F32) + mm(picked, block)).astype(BF16)
            folded = jnp.where(key[m, TOK:] == g.astype(F32), 1.0, 0.0).astype(BF16)
            return total + mm(folded, block)

        total = lax.fori_loop(0, FULL, body, jnp.zeros((TOK, GROUP), F32))
        tail = pl.ds(WIDE, GROUP)
        out[0, :, tail] = (grads[:, tail].astype(F32) + total).astype(BF16)

    tables(0)
    payload(0, x_ref.at[0, 0], False, 0, xs, 0)
    pl.semaphore_wait(barrier, PEERS + 1)
    dispatch(0, 0, xs, 0, range(1, PEERS))
    far = [
        to_partner(0, wg_ref.at[0, 0], wgu.at[1, :, pl.ds(0, FF)]),
        to_partner(1, wu_ref.at[0, 0], wgu.at[1, :, pl.ds(FF, FF)]),
        to_partner(2, wd_ref.at[0, 0], wd.at[pl.ds(FF, FF), :]),
    ]
    for copy in far:
        copy.start()
    payload(0, dy_ref.at[0], True, 1, ws, 0)
    dispatch(1, 1, ws, 0, range(1, PEERS))
    tables(1)
    payload(1, x_ref.at[0, 1], False, 2, xs, 2 * ALL)

    for copy in own:
        copy.wait()
    for copy in far:
        copy.wait()
    arrived(0, xs, 0)
    unfold(xs, 0, ALL)
    pair = [to_partner(3, xs.at[rows_of(0), :], xs.at[rows_of(1), :])]
    pair[-1].start()
    forward(0)
    arrived(1, ws, 0)
    dispatch(3, 2, xs, 2 * ALL, EARLY)
    unfold(ws, 0, ALL)
    pair.append(to_partner(4, ws.at[rows_of(0), :], ws.at[rows_of(1), :]))
    pair[-1].start()
    hidden_terms(0, 0, ALL)
    partials(0, 0, ALL)
    give_back(2, range(1, PEERS))
    pair.append(to_partner(5, g_far.at[0], gs.at[rows_of(1), :]))
    pair[-1].start()
    pair.append(to_partner(6, h_far.at[0], hs.at[rows_of(1), :]))
    pair[-1].start()
    sent(0, send.at[0])

    arrived(2, got, 0)
    dispatch(3, 2, xs, 2 * ALL, LATE)
    combine(0, dy_ref.at[0], first_ref)
    relay = pltpu.make_async_remote_copy(
        src_ref=first_ref.at[0], dst_ref=dy_next, send_sem=y_send, recv_sem=y_recv,
        device_id=before, device_id_type=MESH,
    )
    relay.start()
    relay.wait()

    @pl.when(section == RING - 1)
    def _():
        dy_next[...] = last_ref[...]

    payload(1, dy_next, True, 0, ws, 2 * ALL)
    dispatch(4, 0, ws, 2 * ALL, EARLY)
    dispatch(5, 0, ws, 2 * ALL, LATE)
    sent(2, back)
    arrived(3, xs, 2 * ALL)
    unfold(xs, 2 * ALL, ALL)
    pair.append(to_partner(7, xs.at[rows_of(2), :], xs.at[rows_of(3), :]))
    pair[-1].start()
    forward(1)
    arrived(4, ws, 2 * ALL, ROWS, HALF)
    unfold(ws, 2 * ALL, HALF)
    hidden_terms(1, 0, HALF)
    partials(1, 0, HALF)
    give_back(6, EARLY)
    arrived(5, ws, 2 * ALL, HALF, ALL)
    unfold(ws, 2 * ALL + HALF, HALF)
    pair.append(to_partner(8, ws.at[rows_of(2), :], ws.at[rows_of(3), :]))
    pair[-1].start()
    hidden_terms(1, HALF, HALF)
    pair.append(to_partner(9, g_far.at[1], gs.at[rows_of(3), :]))
    pair[-1].start()
    pair.append(to_partner(10, h_far.at[1], hs.at[rows_of(3), :]))
    pair[-1].start()
    partials(1, HALF, HALF)
    give_back(6, LATE)

    for copy in pair:
        copy.wait()
    h_t[...] = hs[...].astype(F32).T.astype(BF16)

    def stores(d):
        slot = d % 2
        rows = cols(d)
        return [
            pltpu.make_async_copy(
                stage_gu.at[slot, :, pl.ds(0, FF)], gg_ref.at[0, 0, rows, :], osem.at[slot, 0]
            ),
            pltpu.make_async_copy(
                stage_gu.at[slot, :, pl.ds(FF, FF)], gu_ref.at[0, 0, rows, :], osem.at[slot, 1]
            ),
            pltpu.make_async_copy(stage_d.at[slot], gd_ref.at[0, 0, :, rows], osem.at[slot, 2]),
        ]

    def weight_body(d, carry):
        @pl.when(d >= 2)
        def _():
            for copy in stores(d - 2):
                copy.wait()

        slot = d % 2
        value = lax.dot_general(xs[:, cols(d)], gs[...], DOWN, preferred_element_type=F32)
        stage_gu[slot] = value.astype(BF16)
        stage_d[slot] = mm(h_t[...], ws[:, cols(d)]).astype(BF16)
        for copy in stores(d):
            copy.start()
        return carry

    lax.fori_loop(0, D // GROUP, weight_body, 0)

    arrived(6, got, 0)
    combine(1, dy_next, second_ref)
    for d in range(D // GROUP - 2, D // GROUP):
        for copy in stores(d):
            copy.wait()
    sent(1, send.at[1])
    sent(3, send.at[2])
    sent(4, send.at[0], ROWS, HALF)
    sent(5, send.at[0], HALF, ALL)
    sent(6, back)


def place(*refs):
    count = len(refs) // 3
    sources, results, held = refs[:count], refs[count : 2 * count], refs[2 * count : 3 * count]
    come, go = refs[3 * count :]
    reads, writes = [], []
    for source, result, buffer in zip(sources, results, held):
        parts = 4 if source.size > 1 << 20 else 1
        for p in range(parts):
            size = source.shape[-2] // parts
            rows = (0,) * (len(source.shape) - 2) + (pl.ds(p * size, size),)
            n = len(reads)
            reads.append(pltpu.make_async_copy(source.at[rows], buffer.at[rows], come.at[n]))
            writes.append(pltpu.make_async_copy(buffer.at[rows], result.at[rows], go.at[n]))
    for read in reads:
        read.start()
    for read, write in zip(reads, writes):
        read.wait()
        write.start()
    for write in writes:
        write.wait()


def local(saved_inputs, arriving, last_grad, expert_ids, combine, w_gate, w_up, w_down):
    vmem = pl.BlockSpec(memory_space=pltpu.VMEM)
    hbm = pl.BlockSpec(memory_space=pl.ANY)
    grads = jax.ShapeDtypeStruct(arriving.shape, BF16)
    dma = pltpu.SemaphoreType.DMA
    results = pl.pallas_call(
        kernel,
        out_shape=(
            grads,
            grads,
            jax.ShapeDtypeStruct(w_gate.shape, BF16),
            jax.ShapeDtypeStruct(w_up.shape, BF16),
            jax.ShapeDtypeStruct(w_down.shape, BF16),
        ),
        in_specs=[vmem] * 5 + [hbm] * 3,
        out_specs=(vmem, vmem, hbm, hbm, hbm),
        scratch_shapes=[
            pltpu.VMEM((2, D, 2 * FF), BF16),
            pltpu.VMEM((2 * FF, D), BF16),
            pltpu.VMEM((4 * ALL, D), BF16),
            pltpu.VMEM((4 * ALL, D), BF16),
            pltpu.VMEM((4 * ALL, 2 * FF), BF16),
            pltpu.VMEM((4 * ALL, FF), BF16),
            pltpu.VMEM((2, ALL, 2 * FF), BF16),
            pltpu.VMEM((2, ALL, FF), BF16),
            pltpu.VMEM((3, ALL, WIDE), BF16),
            pltpu.VMEM((ALL, WIDE), BF16),
            pltpu.VMEM((ALL, WIDE), BF16),
            pltpu.VMEM((TOK, D), BF16),
            pltpu.VMEM((2, ALL, 2 * FF), F32),
            pltpu.VMEM((ALL, 2 * FF), F32),
            pltpu.VMEM((2, 2 * TOK, ALL), F32),
            pltpu.VMEM((2, ALL, 2 * TOK), F32),
            pltpu.VMEM((2, ALL, 2 * TOK), F32),
            pltpu.VMEM((FF, 4 * ALL), BF16),
            pltpu.VMEM((2, GROUP, 2 * FF), BF16),
            pltpu.VMEM((2, FF, GROUP), BF16),
            dma((7,)),
            dma((7,)),
            dma((3,)),
            dma((11,)),
            dma((11,)),
            dma,
            dma,
            dma((2, 3)),
        ],
        compiler_params=pltpu.CompilerParams(
            collective_id=0, has_side_effects=True, vmem_limit_bytes=63 << 20
        ),
        name="relay_backward",
    )(
        saved_inputs, arriving, last_grad, expert_ids.transpose(0, 3, 1, 2),
        combine.transpose(0, 3, 1, 2), w_gate, w_up, w_down,
    )
    return pl.pallas_call(
        place,
        out_shape=tuple(jax.ShapeDtypeStruct(r.shape, r.dtype) for r in results),
        in_specs=[hbm] * 5,
        out_specs=(hbm,) * 5,
        scratch_shapes=[pltpu.VMEM(r.shape, r.dtype) for r in results] + [dma((14,)), dma((14,))],
        compiler_params=pltpu.CompilerParams(vmem_limit_bytes=63 << 20),
        name="place",
    )(*results)


def solution(mesh):
    return jax.shard_map(
        local,
        mesh=mesh,
        in_specs=(
            P("section", None, "expert", None),
            P("section", "expert", None),
            P("expert", None),
            P("section", None, "expert", None),
            P("section", None, "expert", None),
            P("section", "expert", None, None),
            P("section", "expert", None, None),
            P("section", "expert", None, None),
        ),
        out_specs=(
            P("section", "expert", None),
            P("section", "expert", None),
            P("section", "expert", None, None),
            P("section", "expert", None, None),
            P("section", "expert", None, None),
        ),
        check_vma=False,
    )
```

```python
import jax
import jax.numpy as jnp
from jax import lax
from jax.experimental import pallas as pl
from jax.experimental.pallas import tpu as pltpu
from jax.sharding import PartitionSpec as P

MESH = pl.DeviceIdType.MESH
F32 = jnp.float32
BF16 = jnp.bfloat16

RING = 4
PEERS = RING * RING
ROWS = 16
CAP = 14
GROUP = 256
FULL = 7
WIDE = FULL * GROUP
D = 4096
SIDE = D // 2
BOTH = (0, 1)
TOK = 64
FF = 384
ALL = PEERS * ROWS

STEPS = (
    (0, 0), (2, 2), (1, 0), (-1, 2), (0, 1), (2, 1), (0, -1), (2, -1),
    (1, 2), (-1, 0), (1, 1), (0, 2), (-1, -1), (2, 0), (1, -1), (-1, 1),
)
EARLY, LATE, OTHERS = range(1, 8), range(8, 16), range(1, 16)
HALF = ALL // 2

ACROSS = (((1,), (1,)), ((), ()))
DOWN = (((0,), (0,)), ((), ()))


def mm(a, b):
    return jnp.dot(a, b, preferred_element_type=F32)


def mm_t(a, b):
    return lax.dot_general(a, b, ACROSS, preferred_element_type=F32)


def iota(shape, axis):
    return lax.broadcasted_iota(jnp.int32, shape, axis)


def spread(group, transposed, count):
    to, come = iota((count, count), int(transposed)), iota((count, count), int(not transposed))
    slot = to % ROWS
    late = (slot >= 7).astype(jnp.int32)
    hit = jnp.logical_and(come == to - slot + CAP + late, slot - 7 * late == group)
    return hit.astype(F32).astype(BF16)


def cols(half, group, count=1):
    return pl.ds(pl.multiple_of(half * SIDE + group * GROUP, GROUP), count * GROUP)


def sent_cols(half, group, count=1):
    return pl.ds(pl.multiple_of(half * WIDE + group * GROUP, GROUP), count * GROUP)


def tile(n, size):
    return pl.ds(pl.multiple_of(n * size, size), size)


def kernel(
    x_ref, dy_ref, last_ref, ids_ref, comb_ref, wg_ref, wu_ref, wd_ref,
    first_ref, second_ref, gg_ref, gu_ref, gd_ref,
    wgu, wd, xs, ws, gs, hs, g_far, h_far, send, back, got, dy_next,
    pre, hg, key, key_t, comb_t, h_t,
    ssem, rsem, wsem, pair_send, pair_recv, y_send, y_recv,
):
    section = lax.axis_index("section")
    place = lax.axis_index("expert")
    at_x, at_z, core = place // (2 * RING), (place // 2) % RING, place % 2

    def expert_at(slot, sign):
        dx, dz = (sign * step % RING for step in STEPS[slot])
        return ((at_x + dx) % RING) * RING + (at_z + dz) % RING

    def chip(slot, sign):
        return (section, expert_at(slot, sign) * 2 + core)

    partner = (section, place + 1 - 2 * core)
    before = ((section + RING - 1) % RING, place)
    after = ((section + 1) % RING, place)

    barrier = pltpu.get_barrier_semaphore()
    for slot in range(1, PEERS):
        pl.semaphore_signal(barrier, inc=1, device_id=chip(slot, 1), device_id_type=MESH)
    pl.semaphore_signal(barrier, inc=1, device_id=partner, device_id_type=MESH)
    pl.semaphore_signal(barrier, inc=1, device_id=after, device_id_type=MESH)

    own = [
        pltpu.make_async_copy(wg_ref.at[0, 0], gg_ref.at[0, 0], wsem.at[0]),
        pltpu.make_async_copy(wu_ref.at[0, 0], gu_ref.at[0, 0], wsem.at[1]),
        pltpu.make_async_copy(wd_ref.at[0, 0], gd_ref.at[0, 0], wsem.at[2]),
    ]
    for copy in own:
        copy.start()

    def tables(m):
        shape = (ALL, 2 * TOK)
        row, lane = iota(shape, 0), iota(shape, 1)
        c = row % ROWS
        expert = jnp.concatenate(
            [jnp.full((ROWS, 2 * TOK), expert_at(slot, 1), jnp.int32) for slot in range(PEERS)], axis=0
        )
        named = jnp.zeros(shape, F32)
        combined = jnp.zeros(shape, F32)
        for k in range(3):
            ids = ids_ref[0, k, m : m + 1, :]
            weights = comb_ref[0, k, m : m + 1, :].astype(F32)
            hit = jnp.concatenate([ids, ids], axis=1) == expert
            named = jnp.where(hit, 1.0, named)
            combined = jnp.where(hit, jnp.concatenate([weights, weights], axis=1), combined)
        r2, c2 = iota((2 * TOK, 2 * TOK), 0), iota((2 * TOK, 2 * TOK), 1)
        earlier = (r2 < c2 % TOK).astype(F32).astype(BF16)
        rank = mm(named.astype(BF16), earlier)
        top = lane < TOK
        base = jnp.where(top, c, 7 * (c - CAP)).astype(F32)
        fits = jnp.logical_and(named > 0.5, top == (c < CAP))
        value = jnp.where(fits, rank - base, -100.0)
        key_t[m] = value
        key[m] = value.T
        comb_t[m] = combined

    def payload(m, source, scaled, buf, rows_ref, base, halves=BOTH):
        def body(g, carry):
            data = jnp.concatenate(
                [
                    jnp.concatenate([source[:, cols(h, g)] for h in halves], axis=1),
                    jnp.concatenate([source[:, cols(h, FULL)] for h in halves], axis=1),
                ],
                axis=0,
            )
            lane = iota((ALL, 2 * TOK), 1)
            wanted = jnp.where(lane < TOK, 0, g).astype(F32)
            table = jnp.where(key_t[m] == wanted, comb_t[m] if scaled else 1.0, 0.0)
            value = mm(table.astype(BF16), data).astype(BF16)
            for n, h in enumerate(halves):
                piece = value[:, n * GROUP : (n + 1) * GROUP]
                send[buf, :, sent_cols(h, g)] = piece
                rows_ref[pl.ds(base, ROWS), cols(h, g)] = piece[:ROWS]
            return carry

        lax.fori_loop(0, FULL, body, 0)

    def dispatch(phase, buf, rows_ref, base, slots, halves=BOTH):
        for slot in slots:
            for h in halves:
                pltpu.make_async_remote_copy(
                    src_ref=send.at[buf, pl.ds(slot * ROWS, ROWS), sent_cols(h, 0, FULL)],
                    dst_ref=rows_ref.at[pl.ds(base + slot * ROWS, ROWS), cols(h, 0, FULL)],
                    send_sem=ssem.at[phase],
                    recv_sem=rsem.at[phase],
                    device_id=chip(slot, 1),
                    device_id_type=MESH,
                ).start()

    def settle(sem, slots, halves):
        part = back.at[pl.ds(slots[0] * ROWS, len(slots) * ROWS), pl.ds(0, len(halves) * WIDE)]
        pltpu.make_async_copy(part, part, sem).wait()

    def sent(phase, slots=OTHERS, halves=BOTH):
        settle(ssem.at[phase], slots, halves)

    def arrived(phase, slots=OTHERS, halves=BOTH):
        settle(rsem.at[phase], slots, halves)

    def unfold(ref, base, count, halves=BOTH):
        total = jnp.zeros((count, len(halves) * GROUP), F32)
        rows = pl.ds(base, count)
        for g in range(FULL):
            block = jnp.concatenate([ref[rows, cols(h, g)] for h in halves], axis=1)
            total = total + mm(spread(g, False, count), block)
        for n, h in enumerate(halves):
            ref[rows, cols(h, FULL)] = total[:, n * GROUP : (n + 1) * GROUP].astype(BF16)

    def to_partner(n, src, dst):
        return pltpu.make_async_remote_copy(
            src_ref=src, dst_ref=dst, send_sem=pair_send.at[n], recv_sem=pair_recv.at[n],
            device_id=partner, device_id_type=MESH,
        )

    def rows_of(part):
        return pl.ds(part * ALL, ALL)

    def forward(m):
        base = 2 * m * ALL

        def body(n, carry):
            pre[1, :, tile(n, 256)] = mm(xs[pl.ds(base, ALL), :], wgu[:, tile(n, 256)])
            return carry

        for n in range(3):
            lo, hi = n * 256, (n + 1) * 256
            pieces = [gg_ref[0, 0, :, lo : min(hi, FF)]] if lo < FF else []
            if hi > FF:
                pieces.append(gu_ref[0, 0, :, max(lo - FF, 0) : hi - FF])
            block = pieces[0] if len(pieces) == 1 else jnp.concatenate(pieces, axis=1)
            pre[0, :, lo:hi] = mm(xs[pl.ds(base, ALL), :], block)
        lax.fori_loop(0, 3, body, 0)

    def hidden_part(m, lo, count, h):
        rows, part = pl.ds(2 * m * ALL + lo, count), cols(h, 0, 8)

        for half, weights in ((0, gd_ref.at[0, 0]), (1, wd)):
            value = mm_t(weights[:, part], ws[rows, part]).T
            if h:
                value = value + hg[pl.ds(lo, count), half * FF : (half + 1) * FF]
            hg[pl.ds(lo, count), half * FF : (half + 1) * FF] = value

    def row_terms(m, lo, count):
        base = 2 * m * ALL + lo
        real = iota((count, FF), 0) % ROWS < CAP
        part = pl.ds(lo, count)
        for half in range(2):
            gate, up = pre[half, part, :FF], pre[half, part, FF:]
            grad = hg[part, half * FF : (half + 1) * FF]
            sig = jax.nn.sigmoid(gate)
            active = gate * sig
            hidden = jnp.where(real, active * up, 0.0).astype(BF16)
            gate_rows = grad * up * sig * (1.0 + gate * (1.0 - sig))
            gate_rows = jnp.where(real, gate_rows, 0.0).astype(BF16)
            up_rows = jnp.where(real, grad * active, 0.0).astype(BF16)
            if half == 0:
                gs[pl.ds(base, count), :FF] = gate_rows
                gs[pl.ds(base, count), FF:] = up_rows
                hs[pl.ds(base, count), :] = hidden
            else:
                g_far[m, part, :FF] = gate_rows
                g_far[m, part, FF:] = up_rows
                h_far[m, part, :] = hidden

    def partials(m, lo, count, h):
        def pair_of(n):
            part = cols(h, 2 * n, 2)
            own_part = jnp.concatenate([gg_ref[0, 0, part, :], gu_ref[0, 0, part, :]], axis=1)
            near = mm_t(gs[pl.ds(2 * m * ALL + lo, count), :], own_part)
            return near + mm_t(g_far[m, pl.ds(lo, count), :], wgu[part, :])

        def keep(g, value):
            value = (value + mm(spread(g, True, count), folded)).astype(BF16)
            back[pl.ds(lo, count), sent_cols(h, g)] = value
            if lo == 0:
                got[pl.ds(0, ROWS), sent_cols(h, g)] = value[:ROWS]

        last = pair_of(3)
        folded = last[:, GROUP:].astype(BF16)
        keep(6, last[:, :GROUP])

        def body(n, carry):
            value = pair_of(n)
            keep(2 * n, value[:, :GROUP])
            keep(2 * n + 1, value[:, GROUP:])
            return carry

        lax.fori_loop(0, 3, body, 0)

    def give_back(phase, slots, h):
        for slot in slots:
            pltpu.make_async_remote_copy(
                src_ref=back.at[pl.ds(slot * ROWS, ROWS), sent_cols(h, 0, FULL)],
                dst_ref=got.at[pl.ds(slot * ROWS, ROWS), sent_cols(h, 0, FULL)],
                send_sem=ssem.at[phase],
                recv_sem=rsem.at[phase],
                device_id=chip(slot, -1),
                device_id_type=MESH,
            ).start()

    def combine(m, grads, out, h):
        def body(g, total):
            wanted = jnp.where(iota((2 * TOK, ALL), 0) < TOK, 0, g).astype(F32)
            table = jnp.where(key[m] == wanted, 1.0, 0.0).astype(BF16)
            value = mm(table, got[:, sent_cols(h, g)])
            out[0, :, cols(h, g)] = (grads[:, cols(h, g)].astype(F32) + value[:TOK]).astype(BF16)
            return total + value[TOK:]

        total = lax.fori_loop(0, FULL, body, jnp.zeros((TOK, GROUP), F32))
        tail = cols(h, FULL)
        out[0, :, tail] = (grads[:, tail].astype(F32) + total).astype(BF16)

    tables(0)
    payload(0, x_ref.at[0, 0], False, 0, xs, 0)
    pl.semaphore_wait(barrier, PEERS + 1)
    dispatch(0, 0, xs, 0, OTHERS)
    far = [
        to_partner(0, wg_ref.at[0, 0], wgu.at[:, pl.ds(0, FF)]),
        to_partner(1, wu_ref.at[0, 0], wgu.at[:, pl.ds(FF, FF)]),
        to_partner(2, wd_ref.at[0, 0], wd),
    ]
    for copy in far:
        copy.start()
    payload(0, dy_ref.at[0], True, 1, ws, 0)
    dispatch(1, 1, ws, 0, OTHERS)
    tables(1)
    payload(1, x_ref.at[0, 1], False, 2, xs, 2 * ALL)

    for copy in own:
        copy.wait()
    for copy in far:
        copy.wait()
    arrived(0)
    unfold(xs, 0, ALL)
    pair = [to_partner(3, xs.at[rows_of(0), :], xs.at[rows_of(1), :])]
    pair[-1].start()
    forward(0)
    arrived(1)
    dispatch(4, 2, xs, 2 * ALL, EARLY)
    unfold(ws, 0, ALL)
    pair.append(to_partner(4, ws.at[rows_of(0), :], ws.at[rows_of(1), :]))
    pair[-1].start()
    for h in BOTH:
        hidden_part(0, 0, ALL, h)
    row_terms(0, 0, ALL)
    for h in BOTH:
        partials(0, 0, ALL, h)
        give_back(2 + h, OTHERS, h)
    pair.append(to_partner(5, g_far.at[0], gs.at[rows_of(1), :]))
    pair[-1].start()
    pair.append(to_partner(6, h_far.at[0], hs.at[rows_of(1), :]))
    pair[-1].start()
    sent(0)

    relays = [
        pltpu.make_async_remote_copy(
            src_ref=first_ref.at[0, :, cols(h, 0, 8)], dst_ref=dy_next.at[:, cols(h, 0, 8)],
            send_sem=y_send.at[h], recv_sem=y_recv.at[h], device_id=before, device_id_type=MESH,
        )
        for h in BOTH
    ]

    def take(h):
        relays[h].wait()

        @pl.when(section == RING - 1)
        def _():
            dy_next[:, cols(h, 0, 8)] = last_ref[:, cols(h, 0, 8)]

        payload(1, dy_next, True, 0, ws, 2 * ALL, (h,))

    arrived(2, OTHERS, (0,))
    combine(0, dy_ref.at[0], first_ref, 0)
    relays[0].start()
    take(0)
    dispatch(5, 0, ws, 2 * ALL, OTHERS, (0,))
    arrived(3, OTHERS, (1,))
    combine(0, dy_ref.at[0], first_ref, 1)
    relays[1].start()
    dispatch(4, 2, xs, 2 * ALL, LATE)
    take(1)
    dispatch(6, 0, ws, 2 * ALL, OTHERS, (1,))

    sent(2, OTHERS, (0,))
    sent(3, OTHERS, (1,))
    arrived(4)
    unfold(xs, 2 * ALL, ALL)
    pair.append(to_partner(7, xs.at[rows_of(2), :], xs.at[rows_of(3), :]))
    pair[-1].start()
    forward(1)
    arrived(5, OTHERS, (0,))
    unfold(ws, 2 * ALL, ALL, (0,))
    hidden_part(1, 0, ALL, 0)
    arrived(6, OTHERS, (1,))
    unfold(ws, 2 * ALL, ALL, (1,))
    pair.append(to_partner(8, ws.at[rows_of(2), :], ws.at[rows_of(3), :]))
    pair[-1].start()
    hidden_part(1, 0, ALL, 1)
    row_terms(1, 0, ALL)
    pair.append(to_partner(9, g_far.at[1], gs.at[rows_of(3), :]))
    pair[-1].start()
    pair.append(to_partner(10, h_far.at[1], hs.at[rows_of(3), :]))
    pair[-1].start()
    for h in BOTH:
        partials(1, 0, ALL, h)
        give_back(7 + h, OTHERS, h)

    for copy in pair:
        copy.wait()
    h_t[...] = hs[...].astype(F32).T.astype(BF16)

    def weight_body(d, carry):
        part = tile(d, 512)
        value = lax.dot_general(xs[:, part], gs[...], DOWN, preferred_element_type=F32)
        gg_ref[0, 0, part, :] = value[:, :FF].astype(BF16)
        gu_ref[0, 0, part, :] = value[:, FF:].astype(BF16)
        gd_ref[0, 0, :, part] = mm(h_t[...], ws[:, part]).astype(BF16)
        return carry

    lax.fori_loop(0, D // 512, weight_body, 0)

    for h in BOTH:
        arrived(7 + h, OTHERS, (h,))
        combine(1, dy_next, second_ref, h)
    sent(1)
    sent(4)
    sent(5, OTHERS, (0,))
    sent(6, OTHERS, (1,))
    for h in BOTH:
        sent(7 + h, OTHERS, (h,))


def place(*refs):
    count = (len(refs) - 1) // 2
    copies = []
    for source, result in zip(refs[:count], refs[count:-1]):
        parts = 4 if source.size > 1 << 20 else 1
        for p in range(parts):
            size = source.shape[-2] // parts
            rows = (0,) * (len(source.shape) - 2) + (pl.ds(p * size, size),)
            copies.append(pltpu.make_async_copy(source.at[rows], result.at[rows], refs[-1].at[len(copies)]))
    for copy in copies:
        copy.start()
    for copy in copies:
        copy.wait()


def local(saved_inputs, arriving, last_grad, expert_ids, combine, w_gate, w_up, w_down):
    vmem = pl.BlockSpec(memory_space=pltpu.VMEM)
    hbm = pl.BlockSpec(memory_space=pl.ANY)
    dma = pltpu.SemaphoreType.DMA
    results = pl.pallas_call(
        kernel,
        out_shape=tuple(pltpu.VMEM(a.shape, BF16) for a in (arriving, arriving, w_gate, w_up, w_down)),
        in_specs=[vmem] * 5 + [hbm] * 3,
        out_specs=(vmem,) * 5,
        scratch_shapes=[
            pltpu.VMEM((D, 2 * FF), BF16),
            pltpu.VMEM((FF, D), BF16),
            pltpu.VMEM((4 * ALL, D), BF16),
            pltpu.VMEM((4 * ALL, D), BF16),
            pltpu.VMEM((4 * ALL, 2 * FF), BF16),
            pltpu.VMEM((4 * ALL, FF), BF16),
            pltpu.VMEM((2, ALL, 2 * FF), BF16),
            pltpu.VMEM((2, ALL, FF), BF16),
            pltpu.VMEM((3, ALL, 2 * WIDE), BF16),
            pltpu.VMEM((ALL, 2 * WIDE), BF16),
            pltpu.VMEM((ALL, 2 * WIDE), BF16),
            pltpu.VMEM((TOK, D), BF16),
            pltpu.VMEM((2, ALL, 2 * FF), F32),
            pltpu.VMEM((ALL, 2 * FF), F32),
            pltpu.VMEM((2, 2 * TOK, ALL), F32),
            pltpu.VMEM((2, ALL, 2 * TOK), F32),
            pltpu.VMEM((2, ALL, 2 * TOK), F32),
            pltpu.VMEM((FF, 4 * ALL), BF16),
            dma((9,)),
            dma((9,)),
            dma((3,)),
            dma((11,)),
            dma((11,)),
            dma((2,)),
            dma((2,)),
        ],
        compiler_params=pltpu.CompilerParams(
            collective_id=0, has_side_effects=True, vmem_limit_bytes=50 << 20
        ),
        name="relay_backward",
    )(
        saved_inputs, arriving, last_grad, expert_ids.transpose(0, 3, 1, 2),
        combine.transpose(0, 3, 1, 2), w_gate, w_up, w_down,
    )
    return pl.pallas_call(
        place,
        out_shape=tuple(jax.ShapeDtypeStruct(r.shape, r.dtype) for r in results),
        in_specs=[vmem] * 5,
        out_specs=(hbm,) * 5,
        scratch_shapes=[dma((14,))],
        compiler_params=pltpu.CompilerParams(vmem_limit_bytes=1 << 20),
        name="place",
    )(*[pltpu.with_memory_space_constraint(r, pltpu.VMEM) for r in results])


def solution(mesh):
    return jax.shard_map(
        local,
        mesh=mesh,
        in_specs=(
            P("section", None, "expert", None),
            P("section", "expert", None),
            P("expert", None),
            P("section", None, "expert", None),
            P("section", None, "expert", None),
            P("section", "expert", None, None),
            P("section", "expert", None, None),
            P("section", "expert", None, None),
        ),
        out_specs=(
            P("section", "expert", None),
            P("section", "expert", None),
            P("section", "expert", None, None),
            P("section", "expert", None, None),
            P("section", "expert", None, None),
        ),
        check_vma=False,
    )
```

```python
import jax
import jax.numpy as jnp
from jax import lax
from jax.experimental import pallas as pl
from jax.experimental.pallas import tpu as pltpu
from jax.sharding import PartitionSpec as P

MESH = pl.DeviceIdType.MESH
F32 = jnp.float32
BF16 = jnp.bfloat16

RING = 4
PEERS = RING * RING
ROWS = 16
CAP = 14
GROUP = 256
FULL = 7
WIDE = FULL * GROUP
D = 4096
SIDE = D // 2
BOTH = (0, 1)
TOK = 64
FF = 384
ALL = PEERS * ROWS

STEPS = (
    (0, 0), (2, 2), (1, 0), (-1, 2), (0, 1), (2, 1), (0, -1), (2, -1),
    (1, 2), (-1, 0), (1, 1), (0, 2), (-1, -1), (2, 0), (1, -1), (-1, 1),
)
EARLY, LATE, OTHERS = range(1, 8), range(8, 16), range(1, 16)
HALF = ALL // 2

ACROSS = (((1,), (1,)), ((), ()))
DOWN = (((0,), (0,)), ((), ()))


def mm(a, b):
    return jnp.dot(a, b, preferred_element_type=F32)


def mm_t(a, b):
    return lax.dot_general(a, b, ACROSS, preferred_element_type=F32)


def iota(shape, axis):
    return lax.broadcasted_iota(jnp.int32, shape, axis)


def spread(group, transposed, count):
    to, come = iota((count, count), int(transposed)), iota((count, count), int(not transposed))
    slot = to % ROWS
    late = (slot >= 7).astype(jnp.int32)
    hit = jnp.logical_and(come == to - slot + CAP + late, slot - 7 * late == group)
    return hit.astype(F32).astype(BF16)


def cols(half, group, count=1):
    return pl.ds(pl.multiple_of(half * SIDE + group * GROUP, GROUP), count * GROUP)


def sent_cols(half, group, count=1):
    return pl.ds(pl.multiple_of(half * WIDE + group * GROUP, GROUP), count * GROUP)


def tile(n, size):
    return pl.ds(pl.multiple_of(n * size, size), size)


def combine(table_of, got, grads, out, h):
    def body(g, total):
        wanted = jnp.where(iota((2 * TOK, ALL), 0) < TOK, 0, g).astype(F32)
        table = jnp.where(table_of[...] == wanted, 1.0, 0.0).astype(BF16)
        value = mm(table, got[:, sent_cols(h, g)])
        out[:, cols(h, g)] = (grads[:, cols(h, g)].astype(F32) + value[:TOK]).astype(BF16)
        return total + value[TOK:]

    total = lax.fori_loop(0, FULL, body, jnp.zeros((TOK, GROUP), F32))
    tail = cols(h, FULL)
    out[:, tail] = (grads[:, tail].astype(F32) + total).astype(BF16)


def kernel(
    x_ref, dy_ref, last_ref, ids_ref, comb_ref, wg_ref, wu_ref, wd_ref,
    first_ref, gg_ref, gu_ref, gd_ref, got, dy_next, key,
    x_in, dy_in, last_in, wgu, wd, xs, ws, gs, hs, g_far, h_far, send, back,
    pre, hg, key_t, comb_t, h_t,
    ssem, rsem, isem, wsem, pair_send, pair_recv, y_send, y_recv,
):
    section = lax.axis_index("section")
    place = lax.axis_index("expert")
    at_x, at_z, core = place // (2 * RING), (place // 2) % RING, place % 2

    def expert_at(slot, sign):
        dx, dz = (sign * step % RING for step in STEPS[slot])
        return ((at_x + dx) % RING) * RING + (at_z + dz) % RING

    def chip(slot, sign):
        return (section, expert_at(slot, sign) * 2 + core)

    partner = (section, place + 1 - 2 * core)
    before = ((section + RING - 1) % RING, place)
    after = ((section + 1) % RING, place)

    barrier = pltpu.get_barrier_semaphore()
    for slot in range(1, PEERS):
        pl.semaphore_signal(barrier, inc=1, device_id=chip(slot, 1), device_id_type=MESH)
    pl.semaphore_signal(barrier, inc=1, device_id=partner, device_id_type=MESH)
    pl.semaphore_signal(barrier, inc=1, device_id=after, device_id_type=MESH)

    load = [
        pltpu.make_async_copy(x_ref.at[0, 0], x_in.at[0], isem.at[0]),
        pltpu.make_async_copy(dy_ref.at[0], dy_in, isem.at[1]),
        pltpu.make_async_copy(x_ref.at[0, 1], x_in.at[1], isem.at[2]),
        pltpu.make_async_copy(last_ref, last_in, isem.at[3]),
    ]
    load[0].start()

    own = [
        pltpu.make_async_copy(wg_ref.at[0, 0], gg_ref.at[0, 0], wsem.at[0]),
        pltpu.make_async_copy(wu_ref.at[0, 0], gu_ref.at[0, 0], wsem.at[1]),
        pltpu.make_async_copy(wd_ref.at[0, 0], gd_ref.at[0, 0], wsem.at[2]),
    ]

    def tables(m):
        shape = (ALL, 2 * TOK)
        row, lane = iota(shape, 0), iota(shape, 1)
        c = row % ROWS
        expert = jnp.concatenate(
            [jnp.full((ROWS, 2 * TOK), expert_at(slot, 1), jnp.int32) for slot in range(PEERS)], axis=0
        )
        named = jnp.zeros(shape, F32)
        combined = jnp.zeros(shape, F32)
        for k in range(3):
            ids = ids_ref[0, k, m : m + 1, :]
            weights = comb_ref[0, k, m : m + 1, :].astype(F32)
            hit = jnp.concatenate([ids, ids], axis=1) == expert
            named = jnp.where(hit, 1.0, named)
            combined = jnp.where(hit, jnp.concatenate([weights, weights], axis=1), combined)
        r2, c2 = iota((2 * TOK, 2 * TOK), 0), iota((2 * TOK, 2 * TOK), 1)
        earlier = (r2 < c2 % TOK).astype(F32).astype(BF16)
        rank = mm(named.astype(BF16), earlier)
        top = lane < TOK
        base = jnp.where(top, c, 7 * (c - CAP)).astype(F32)
        fits = jnp.logical_and(named > 0.5, top == (c < CAP))
        value = jnp.where(fits, rank - base, -100.0)
        key_t[m] = value
        key[m] = value.T
        comb_t[m] = combined

    def payload(m, source, scaled, buf, rows_ref, base, halves=BOTH, lo=0, count=ALL):
        def body(g, carry):
            data = jnp.concatenate(
                [
                    jnp.concatenate([source[:, cols(h, g)] for h in halves], axis=1),
                    jnp.concatenate([source[:, cols(h, FULL)] for h in halves], axis=1),
                ],
                axis=0,
            )
            lane = iota((count, 2 * TOK), 1)
            rows = pl.ds(lo, count)
            wanted = jnp.where(lane < TOK, 0, g).astype(F32)
            table = jnp.where(key_t[m, rows, :] == wanted, comb_t[m, rows, :] if scaled else 1.0, 0.0)
            value = mm(table.astype(BF16), data).astype(BF16)
            for n, h in enumerate(halves):
                piece = value[:, n * GROUP : (n + 1) * GROUP]
                send[buf, rows, sent_cols(h, g)] = piece
                if lo == 0:
                    rows_ref[pl.ds(base, ROWS), cols(h, g)] = piece[:ROWS]
            return carry

        lax.fori_loop(0, FULL, body, 0)

    def dispatch(phase, buf, rows_ref, base, slots, halves=BOTH):
        for slot in slots:
            for h in halves:
                pltpu.make_async_remote_copy(
                    src_ref=send.at[buf, pl.ds(slot * ROWS, ROWS), sent_cols(h, 0, FULL)],
                    dst_ref=rows_ref.at[pl.ds(base + slot * ROWS, ROWS), cols(h, 0, FULL)],
                    send_sem=ssem.at[phase],
                    recv_sem=rsem.at[phase],
                    device_id=chip(slot, 1),
                    device_id_type=MESH,
                ).start()

    def settle(sem, slots, halves):
        part = back.at[pl.ds(slots[0] * ROWS, len(slots) * ROWS), pl.ds(0, len(halves) * WIDE)]
        pltpu.make_async_copy(part, part, sem).wait()

    def sent(phase, slots=OTHERS, halves=BOTH):
        settle(ssem.at[phase], slots, halves)

    def arrived(phase, slots=OTHERS, halves=BOTH):
        settle(rsem.at[phase], slots, halves)

    def unfold(ref, base, count, halves=BOTH):
        total = jnp.zeros((count, len(halves) * GROUP), F32)
        rows = pl.ds(base, count)
        for g in range(FULL):
            block = jnp.concatenate([ref[rows, cols(h, g)] for h in halves], axis=1)
            total = total + mm(spread(g, False, count), block)
        for n, h in enumerate(halves):
            ref[rows, cols(h, FULL)] = total[:, n * GROUP : (n + 1) * GROUP].astype(BF16)

    def to_partner(n, src, dst):
        return pltpu.make_async_remote_copy(
            src_ref=src, dst_ref=dst, send_sem=pair_send.at[n], recv_sem=pair_recv.at[n],
            device_id=partner, device_id_type=MESH,
        )

    def rows_of(part):
        return pl.ds(part * ALL, ALL)

    def forward(m):
        base = 2 * m * ALL

        def body(n, carry):
            pre[1, :, tile(n, 256)] = mm(xs[pl.ds(base, ALL), :], wgu[:, tile(n, 256)])
            return carry

        for n in range(3):
            lo, hi = n * 256, (n + 1) * 256
            pieces = [gg_ref[0, 0, :, lo : min(hi, FF)]] if lo < FF else []
            if hi > FF:
                pieces.append(gu_ref[0, 0, :, max(lo - FF, 0) : hi - FF])
            block = pieces[0] if len(pieces) == 1 else jnp.concatenate(pieces, axis=1)
            pre[0, :, lo:hi] = mm(xs[pl.ds(base, ALL), :], block)
        lax.fori_loop(0, 3, body, 0)

    def hidden_part(m, lo, count, h):
        rows, part = pl.ds(2 * m * ALL + lo, count), cols(h, 0, 8)

        for half, weights in ((0, gd_ref.at[0, 0]), (1, wd)):
            value = mm_t(weights[:, part], ws[rows, part]).T
            if h:
                value = value + hg[pl.ds(lo, count), half * FF : (half + 1) * FF]
            hg[pl.ds(lo, count), half * FF : (half + 1) * FF] = value

    def row_terms(m, lo, count):
        base = 2 * m * ALL + lo
        real = iota((count, FF), 0) % ROWS < CAP
        part = pl.ds(lo, count)
        for half in range(2):
            gate, up = pre[half, part, :FF], pre[half, part, FF:]
            grad = hg[part, half * FF : (half + 1) * FF]
            sig = jax.nn.sigmoid(gate)
            active = gate * sig
            hidden = jnp.where(real, active * up, 0.0).astype(BF16)
            gate_rows = grad * up * sig * (1.0 + gate * (1.0 - sig))
            gate_rows = jnp.where(real, gate_rows, 0.0).astype(BF16)
            up_rows = jnp.where(real, grad * active, 0.0).astype(BF16)
            if half == 0:
                gs[pl.ds(base, count), :FF] = gate_rows
                gs[pl.ds(base, count), FF:] = up_rows
                hs[pl.ds(base, count), :] = hidden
            else:
                g_far[m, part, :FF] = gate_rows
                g_far[m, part, FF:] = up_rows
                h_far[m, part, :] = hidden

    def partials(m, lo, count, h, phase):
        def pair_of(n):
            part = cols(h, 2 * n, 2)
            own_part = jnp.concatenate([gg_ref[0, 0, part, :], gu_ref[0, 0, part, :]], axis=1)
            near = mm_t(gs[pl.ds(2 * m * ALL + lo, count), :], own_part)
            return near + mm_t(g_far[m, pl.ds(lo, count), :], wgu[part, :])

        def keep(g, value):
            value = (value + mm(spread(g, True, count), folded)).astype(BF16)
            back[pl.ds(lo, count), sent_cols(h, g)] = value
            if lo == 0:
                got[pl.ds(0, ROWS), sent_cols(h, g)] = value[:ROWS]

        last = pair_of(3)
        folded = last[:, GROUP:].astype(BF16)
        keep(6, last[:, :GROUP])

        def both(n):
            value = pair_of(n)
            keep(2 * n, value[:, :GROUP])
            keep(2 * n + 1, value[:, GROUP:])

        both(2)
        give_back(phase, h, 4, 3)
        both(1)
        both(0)
        give_back(phase, h, 0, 4)

    def give_back(phase, h, group, count):
        for slot in OTHERS:
            pltpu.make_async_remote_copy(
                src_ref=back.at[pl.ds(slot * ROWS, ROWS), sent_cols(h, group, count)],
                dst_ref=got.at[pl.ds(slot * ROWS, ROWS), sent_cols(h, group, count)],
                send_sem=ssem.at[phase],
                recv_sem=rsem.at[phase],
                device_id=chip(slot, -1),
                device_id_type=MESH,
            ).start()

    tables(0)
    load[0].wait()
    for copy in load[1:] + own:
        copy.start()
    payload(0, x_in.at[0], False, 0, xs, 0, BOTH, 0, HALF)
    pl.semaphore_wait(barrier, PEERS + 1)
    dispatch(0, 0, xs, 0, EARLY)
    payload(0, x_in.at[0], False, 0, xs, 0, BOTH, HALF, HALF)
    dispatch(0, 0, xs, 0, LATE)
    far = [
        to_partner(0, wg_ref.at[0, 0], wgu.at[:, pl.ds(0, FF)]),
        to_partner(1, wu_ref.at[0, 0], wgu.at[:, pl.ds(FF, FF)]),
        to_partner(2, wd_ref.at[0, 0], wd),
    ]
    load[1].wait()
    payload(0, dy_in, True, 1, ws, 0)
    dispatch(1, 1, ws, 0, OTHERS)
    for copy in far:
        copy.start()
    tables(1)
    load[2].wait()
    load[3].wait()
    payload(1, x_in.at[1], False, 2, xs, 2 * ALL)

    for copy in own:
        copy.wait()
    for copy in far:
        copy.wait()
    arrived(0)
    unfold(xs, 0, ALL)
    pair = [to_partner(3, xs.at[rows_of(0), :], xs.at[rows_of(1), :])]
    pair[-1].start()
    forward(0)
    arrived(1)
    dispatch(4, 2, xs, 2 * ALL, EARLY)
    unfold(ws, 0, ALL)
    pair.append(to_partner(4, ws.at[rows_of(0), :], ws.at[rows_of(1), :]))
    pair[-1].start()
    for h in BOTH:
        hidden_part(0, 0, ALL, h)
    row_terms(0, 0, ALL)
    for h in BOTH:
        partials(0, 0, ALL, h, 2 + h)
    pair.append(to_partner(5, g_far.at[0], gs.at[rows_of(1), :]))
    pair[-1].start()
    pair.append(to_partner(6, h_far.at[0], hs.at[rows_of(1), :]))
    pair[-1].start()
    sent(0)

    relays = [
        pltpu.make_async_remote_copy(
            src_ref=first_ref.at[0, :, cols(h, 0, 8)], dst_ref=dy_next.at[:, cols(h, 0, 8)],
            send_sem=y_send.at[h], recv_sem=y_recv.at[h], device_id=before, device_id_type=MESH,
        )
        for h in BOTH
    ]

    def take(h):
        relays[h].wait()

        @pl.when(section == RING - 1)
        def _():
            dy_next[:, cols(h, 0, 8)] = last_in[:, cols(h, 0, 8)]

        payload(1, dy_next, True, 0, ws, 2 * ALL, (h,))

    dispatch(4, 2, xs, 2 * ALL, LATE)
    arrived(2, OTHERS, (0,))
    combine(key.at[0], got, dy_in, first_ref.at[0], 0)
    relays[0].start()
    take(0)
    dispatch(5, 0, ws, 2 * ALL, OTHERS, (0,))
    arrived(3, OTHERS, (1,))
    combine(key.at[0], got, dy_in, first_ref.at[0], 1)
    relays[1].start()
    take(1)
    dispatch(6, 0, ws, 2 * ALL, OTHERS, (1,))

    sent(2, OTHERS, (0,))
    sent(3, OTHERS, (1,))
    arrived(5, OTHERS, (0,))
    unfold(ws, 2 * ALL, ALL, (0,))
    hidden_part(1, 0, ALL, 0)
    arrived(4)
    unfold(xs, 2 * ALL, ALL)
    pair.append(to_partner(7, xs.at[rows_of(2), :], xs.at[rows_of(3), :]))
    pair[-1].start()
    forward(1)
    arrived(6, OTHERS, (1,))
    unfold(ws, 2 * ALL, ALL, (1,))
    pair.append(to_partner(8, ws.at[rows_of(2), :], ws.at[rows_of(3), :]))
    pair[-1].start()
    hidden_part(1, 0, ALL, 1)
    row_terms(1, 0, ALL)
    pair.append(to_partner(9, g_far.at[1], gs.at[rows_of(3), :]))
    pair[-1].start()
    pair.append(to_partner(10, h_far.at[1], hs.at[rows_of(3), :]))
    pair[-1].start()
    for h in BOTH:
        partials(1, 0, ALL, h, 8 + h)

    for copy in pair:
        copy.wait()
    h_t[...] = hs[...].astype(F32).T.astype(BF16)

    def weight_body(d, carry):
        part = tile(d, 512)
        value = lax.dot_general(xs[:, part], gs[...], DOWN, preferred_element_type=F32)
        gg_ref[0, 0, part, :] = value[:, :FF].astype(BF16)
        gu_ref[0, 0, part, :] = value[:, FF:].astype(BF16)
        gd_ref[0, 0, :, part] = mm(h_t[...], ws[:, part]).astype(BF16)
        return carry

    lax.fori_loop(0, D // 512, weight_body, 0)

    for h in BOTH:
        arrived(8 + h, OTHERS, (h,))
    sent(1)
    sent(4)
    sent(5, OTHERS, (0,))
    sent(6, OTHERS, (1,))
    for h in BOTH:
        sent(8 + h, OTHERS, (h,))


def finish(
    first_ref, gg_ref, gu_ref, gd_ref, got, dy_next, key,
    first_out, second_out, gg_out, gu_out, gd_out, second, sem,
):
    copies = []

    def write(source, result):
        copies.append(pltpu.make_async_copy(source, result, sem.at[len(copies)]))
        copies[-1].start()

    for source, result in ((gg_ref, gg_out), (gu_ref, gu_out), (gd_ref, gd_out)):
        for p in range(4):
            rows = tile(p, source.shape[2] // 4)
            write(source.at[0, 0, rows, :], result.at[0, 0, rows, :])
    write(first_ref, first_out)
    for h in BOTH:
        combine(key.at[1], got, dy_next, second, h)
        write(second.at[:, cols(h, 0, 8)], second_out.at[0, :, cols(h, 0, 8)])
    for copy in copies:
        copy.wait()


def local(saved_inputs, arriving, last_grad, expert_ids, combine, w_gate, w_up, w_down):
    vmem = pl.BlockSpec(memory_space=pltpu.VMEM)
    hbm = pl.BlockSpec(memory_space=pl.ANY)
    dma = pltpu.SemaphoreType.DMA
    kept = [(a.shape, BF16) for a in (arriving, w_gate, w_up, w_down)]
    kept += [((ALL, 2 * WIDE), BF16), ((TOK, D), BF16), ((2, 2 * TOK, ALL), F32)]
    results = pl.pallas_call(
        kernel,
        out_shape=tuple(pltpu.VMEM(*k) for k in kept),
        in_specs=[hbm] * 3 + [vmem] * 2 + [hbm] * 3,
        out_specs=(vmem,) * 7,
        scratch_shapes=[
            pltpu.VMEM((2, TOK, D), BF16),
            pltpu.VMEM((TOK, D), BF16),
            pltpu.VMEM((TOK, D), BF16),
            pltpu.VMEM((D, 2 * FF), BF16),
            pltpu.VMEM((FF, D), BF16),
            pltpu.VMEM((4 * ALL, D), BF16),
            pltpu.VMEM((4 * ALL, D), BF16),
            pltpu.VMEM((4 * ALL, 2 * FF), BF16),
            pltpu.VMEM((4 * ALL, FF), BF16),
            pltpu.VMEM((2, ALL, 2 * FF), BF16),
            pltpu.VMEM((2, ALL, FF), BF16),
            pltpu.VMEM((3, ALL, 2 * WIDE), BF16),
            pltpu.VMEM((ALL, 2 * WIDE), BF16),
            pltpu.VMEM((2, ALL, 2 * FF), F32),
            pltpu.VMEM((ALL, 2 * FF), F32),
            pltpu.VMEM((2, ALL, 2 * TOK), F32),
            pltpu.VMEM((2, ALL, 2 * TOK), F32),
            pltpu.VMEM((FF, 4 * ALL), BF16),
            dma((10,)),
            dma((10,)),
            dma((4,)),
            dma((3,)),
            dma((11,)),
            dma((11,)),
            dma((2,)),
            dma((2,)),
        ],
        compiler_params=pltpu.CompilerParams(
            collective_id=0, has_side_effects=True, vmem_limit_bytes=50 << 20
        ),
        name="relay_backward",
    )(
        saved_inputs, arriving, last_grad, expert_ids.transpose(0, 3, 1, 2),
        combine.transpose(0, 3, 1, 2), w_gate, w_up, w_down,
    )
    return pl.pallas_call(
        finish,
        out_shape=tuple(
            jax.ShapeDtypeStruct(a.shape, BF16) for a in (arriving, arriving, w_gate, w_up, w_down)
        ),
        in_specs=[vmem] * 7,
        out_specs=(hbm,) * 5,
        scratch_shapes=[pltpu.VMEM((TOK, D), BF16), dma((15,))],
        compiler_params=pltpu.CompilerParams(vmem_limit_bytes=4 << 20),
        name="write_results",
    )(*[pltpu.with_memory_space_constraint(r, pltpu.VMEM) for r in results])


def solution(mesh):
    return jax.shard_map(
        local,
        mesh=mesh,
        in_specs=(
            P("section", None, "expert", None),
            P("section", "expert", None),
            P("expert", None),
            P("section", None, "expert", None),
            P("section", None, "expert", None),
            P("section", "expert", None, None),
            P("section", "expert", None, None),
            P("section", "expert", None, None),
        ),
        out_specs=(
            P("section", "expert", None),
            P("section", "expert", None),
            P("section", "expert", None, None),
            P("section", "expert", None, None),
            P("section", "expert", None, None),
        ),
        check_vma=False,
    )
```

```python
import jax
import jax.numpy as jnp
from jax import lax
from jax.experimental import pallas as pl
from jax.experimental.pallas import tpu as pltpu
from jax.sharding import PartitionSpec as P

MESH = pl.DeviceIdType.MESH
F32 = jnp.float32
BF16 = jnp.bfloat16

RING = 4
PEERS = RING * RING
ROWS = 16
CAP = 14
GROUP = 256
FULL = 7
WIDE = FULL * GROUP
D = 4096
SIDE = D // 2
BOTH = (0, 1)
TOK = 64
FF = 384
ALL = PEERS * ROWS

STEPS = (
    (0, 0), (2, 2), (1, 0), (-1, 2), (0, 1), (2, 1), (0, -1), (2, -1),
    (1, 2), (-1, 0), (1, 1), (0, 2), (-1, -1), (2, 0), (1, -1), (-1, 1),
)
EARLY, LATE, OTHERS = range(1, 8), range(8, 16), range(1, 16)
HALF = ALL // 2

ACROSS = (((1,), (1,)), ((), ()))
DOWN = (((0,), (0,)), ((), ()))


def mm(a, b):
    return jnp.dot(a, b, preferred_element_type=F32)


def mm_t(a, b):
    return lax.dot_general(a, b, ACROSS, preferred_element_type=F32)


def iota(shape, axis):
    return lax.broadcasted_iota(jnp.int32, shape, axis)


def spread(group, transposed, count):
    to, come = iota((count, count), int(transposed)), iota((count, count), int(not transposed))
    slot = to % ROWS
    late = (slot >= 7).astype(jnp.int32)
    hit = jnp.logical_and(come == to - slot + CAP + late, slot - 7 * late == group)
    return hit.astype(F32).astype(BF16)


def cols(half, group, count=1):
    return pl.ds(pl.multiple_of(half * SIDE + group * GROUP, GROUP), count * GROUP)


def sent_cols(half, group, count=1):
    return pl.ds(pl.multiple_of(half * WIDE + group * GROUP, GROUP), count * GROUP)


def tile(n, size):
    return pl.ds(pl.multiple_of(n * size, size), size)


def combine(table_of, got, grads, out, h):
    def body(g, total):
        wanted = jnp.where(iota((2 * TOK, ALL), 0) < TOK, 0, g).astype(F32)
        table = jnp.where(table_of[...] == wanted, 1.0, 0.0).astype(BF16)
        value = mm(table, got[:, sent_cols(h, g)])
        out[:, cols(h, g)] = (grads[:, cols(h, g)].astype(F32) + value[:TOK]).astype(BF16)
        return total + value[TOK:]

    total = lax.fori_loop(0, FULL, body, jnp.zeros((TOK, GROUP), F32), unroll=True)
    tail = cols(h, FULL)
    out[:, tail] = (grads[:, tail].astype(F32) + total).astype(BF16)


def kernel(
    x_ref, dy_ref, last_ref, ids_ref, comb_ref, wg_ref, wu_ref, wd_ref,
    first_ref, gg_ref, gu_ref, gd_ref, got, dy_next, key,
    x_in, dy_in, last_in, wgu, wd, xs, ws, gs, hs, g_far, h_far, send, back,
    pre, hg, key_t, comb_t, h_t,
    ssem, rsem, isem, wsem, pair_send, pair_recv, y_send, y_recv,
):
    section = lax.axis_index("section")
    place = lax.axis_index("expert")
    at_x, at_z, core = place // (2 * RING), (place // 2) % RING, place % 2

    def expert_at(slot, sign):
        dx, dz = (sign * step % RING for step in STEPS[slot])
        return ((at_x + dx) % RING) * RING + (at_z + dz) % RING

    def chip(slot, sign):
        return (section, expert_at(slot, sign) * 2 + core)

    partner = (section, place + 1 - 2 * core)
    before = ((section + RING - 1) % RING, place)
    after = ((section + 1) % RING, place)

    barrier = pltpu.get_barrier_semaphore()
    for slot in range(1, PEERS):
        pl.semaphore_signal(barrier, inc=1, device_id=chip(slot, 1), device_id_type=MESH)
    pl.semaphore_signal(barrier, inc=1, device_id=partner, device_id_type=MESH)
    pl.semaphore_signal(barrier, inc=1, device_id=after, device_id_type=MESH)

    load = [
        pltpu.make_async_copy(x_ref.at[0, 0], x_in.at[0], isem.at[0]),
        pltpu.make_async_copy(dy_ref.at[0], dy_in, isem.at[1]),
        pltpu.make_async_copy(x_ref.at[0, 1], x_in.at[1], isem.at[2]),
        pltpu.make_async_copy(last_ref, last_in, isem.at[3]),
    ]
    load[0].start()

    own = [
        pltpu.make_async_copy(wg_ref.at[0, 0], gg_ref.at[0, 0], wsem.at[0]),
        pltpu.make_async_copy(wu_ref.at[0, 0], gu_ref.at[0, 0], wsem.at[1]),
        pltpu.make_async_copy(wd_ref.at[0, 0], gd_ref.at[0, 0], wsem.at[2]),
    ]

    def tables(m):
        shape = (ALL, 2 * TOK)
        row, lane = iota(shape, 0), iota(shape, 1)
        c = row % ROWS
        expert = jnp.concatenate(
            [jnp.full((ROWS, 2 * TOK), expert_at(slot, 1), jnp.int32) for slot in range(PEERS)], axis=0
        )
        named = jnp.zeros(shape, F32)
        combined = jnp.zeros(shape, F32)
        for k in range(3):
            ids = ids_ref[0, k, m : m + 1, :]
            weights = comb_ref[0, k, m : m + 1, :].astype(F32)
            hit = jnp.concatenate([ids, ids], axis=1) == expert
            named = jnp.where(hit, 1.0, named)
            combined = jnp.where(hit, jnp.concatenate([weights, weights], axis=1), combined)
        r2, c2 = iota((2 * TOK, 2 * TOK), 0), iota((2 * TOK, 2 * TOK), 1)
        earlier = (r2 < c2 % TOK).astype(F32).astype(BF16)
        rank = mm(named.astype(BF16), earlier)
        top = lane < TOK
        base = jnp.where(top, c, 7 * (c - CAP)).astype(F32)
        fits = jnp.logical_and(named > 0.5, top == (c < CAP))
        value = jnp.where(fits, rank - base, -100.0)
        key_t[m] = value
        key[m] = value.T
        comb_t[m] = combined

    def payload(m, source, scaled, buf, rows_ref, base, halves=BOTH, lo=0, count=ALL):
        def body(g, carry):
            data = jnp.concatenate(
                [
                    jnp.concatenate([source[:, cols(h, g)] for h in halves], axis=1),
                    jnp.concatenate([source[:, cols(h, FULL)] for h in halves], axis=1),
                ],
                axis=0,
            )
            lane = iota((count, 2 * TOK), 1)
            rows = pl.ds(lo, count)
            wanted = jnp.where(lane < TOK, 0, g).astype(F32)
            table = jnp.where(key_t[m, rows, :] == wanted, comb_t[m, rows, :] if scaled else 1.0, 0.0)
            value = mm(table.astype(BF16), data).astype(BF16)
            for n, h in enumerate(halves):
                piece = value[:, n * GROUP : (n + 1) * GROUP]
                send[buf, rows, sent_cols(h, g)] = piece
                if lo == 0:
                    rows_ref[pl.ds(base, ROWS), cols(h, g)] = piece[:ROWS]
            return carry

        lax.fori_loop(0, FULL, body, 0, unroll=True)

    def dispatch(phase, buf, rows_ref, base, slots, halves=BOTH):
        for slot in slots:
            for h in halves:
                pltpu.make_async_remote_copy(
                    src_ref=send.at[buf, pl.ds(slot * ROWS, ROWS), sent_cols(h, 0, FULL)],
                    dst_ref=rows_ref.at[pl.ds(base + slot * ROWS, ROWS), cols(h, 0, FULL)],
                    send_sem=ssem.at[phase],
                    recv_sem=rsem.at[phase],
                    device_id=chip(slot, 1),
                    device_id_type=MESH,
                ).start()

    def settle(sem, slots, halves):
        part = back.at[pl.ds(slots[0] * ROWS, len(slots) * ROWS), pl.ds(0, len(halves) * WIDE)]
        pltpu.make_async_copy(part, part, sem).wait()

    def sent(phase, slots=OTHERS, halves=BOTH):
        settle(ssem.at[phase], slots, halves)

    def arrived(phase, slots=OTHERS, halves=BOTH):
        settle(rsem.at[phase], slots, halves)

    def unfold(ref, base, count, halves=BOTH):
        total = jnp.zeros((count, len(halves) * GROUP), F32)
        rows = pl.ds(base, count)
        for g in range(FULL):
            block = jnp.concatenate([ref[rows, cols(h, g)] for h in halves], axis=1)
            total = total + mm(spread(g, False, count), block)
        for n, h in enumerate(halves):
            ref[rows, cols(h, FULL)] = total[:, n * GROUP : (n + 1) * GROUP].astype(BF16)

    def to_partner(n, src, dst):
        return pltpu.make_async_remote_copy(
            src_ref=src, dst_ref=dst, send_sem=pair_send.at[n], recv_sem=pair_recv.at[n],
            device_id=partner, device_id_type=MESH,
        )

    def rows_of(part):
        return pl.ds(part * ALL, ALL)

    def forward(m):
        base = 2 * m * ALL

        def body(n, carry):
            pre[1, :, tile(n, 256)] = mm(xs[pl.ds(base, ALL), :], wgu[:, tile(n, 256)])
            return carry

        for n in range(3):
            lo, hi = n * 256, (n + 1) * 256
            pieces = [gg_ref[0, 0, :, lo : min(hi, FF)]] if lo < FF else []
            if hi > FF:
                pieces.append(gu_ref[0, 0, :, max(lo - FF, 0) : hi - FF])
            block = pieces[0] if len(pieces) == 1 else jnp.concatenate(pieces, axis=1)
            pre[0, :, lo:hi] = mm(xs[pl.ds(base, ALL), :], block)
        lax.fori_loop(0, 3, body, 0)

    def hidden_part(m, lo, count, h):
        rows, part = pl.ds(2 * m * ALL + lo, count), cols(h, 0, 8)

        for half, weights in ((0, gd_ref.at[0, 0]), (1, wd)):
            value = mm_t(weights[:, part], ws[rows, part]).T
            if h:
                value = value + hg[pl.ds(lo, count), half * FF : (half + 1) * FF]
            hg[pl.ds(lo, count), half * FF : (half + 1) * FF] = value

    def row_terms(m, lo, count):
        base = 2 * m * ALL + lo
        real = iota((count, FF), 0) % ROWS < CAP
        part = pl.ds(lo, count)
        for half in range(2):
            gate, up = pre[half, part, :FF], pre[half, part, FF:]
            grad = hg[part, half * FF : (half + 1) * FF]
            sig = jax.nn.sigmoid(gate)
            active = gate * sig
            hidden = jnp.where(real, active * up, 0.0).astype(BF16)
            gate_rows = grad * up * sig * (1.0 + gate * (1.0 - sig))
            gate_rows = jnp.where(real, gate_rows, 0.0).astype(BF16)
            up_rows = jnp.where(real, grad * active, 0.0).astype(BF16)
            if half == 0:
                gs[pl.ds(base, count), :FF] = gate_rows
                gs[pl.ds(base, count), FF:] = up_rows
                hs[pl.ds(base, count), :] = hidden
            else:
                g_far[m, part, :FF] = gate_rows
                g_far[m, part, FF:] = up_rows
                h_far[m, part, :] = hidden

    def partials(m, lo, count, h, phase):
        def pair_of(n):
            part = cols(h, 2 * n, 2)
            own_part = jnp.concatenate([gg_ref[0, 0, part, :], gu_ref[0, 0, part, :]], axis=1)
            near = mm_t(gs[pl.ds(2 * m * ALL + lo, count), :], own_part)
            return near + mm_t(g_far[m, pl.ds(lo, count), :], wgu[part, :])

        def keep(g, value):
            value = (value + mm(spread(g, True, count), folded)).astype(BF16)
            back[pl.ds(lo, count), sent_cols(h, g)] = value
            if lo == 0:
                got[pl.ds(0, ROWS), sent_cols(h, g)] = value[:ROWS]

        last = pair_of(3)
        folded = last[:, GROUP:].astype(BF16)
        keep(6, last[:, :GROUP])

        def both(n):
            value = pair_of(n)
            keep(2 * n, value[:, :GROUP])
            keep(2 * n + 1, value[:, GROUP:])

        both(2)
        give_back(phase, h, 4, 3)
        both(1)
        both(0)
        give_back(phase, h, 0, 4)

    def give_back(phase, h, group, count):
        for slot in OTHERS:
            pltpu.make_async_remote_copy(
                src_ref=back.at[pl.ds(slot * ROWS, ROWS), sent_cols(h, group, count)],
                dst_ref=got.at[pl.ds(slot * ROWS, ROWS), sent_cols(h, group, count)],
                send_sem=ssem.at[phase],
                recv_sem=rsem.at[phase],
                device_id=chip(slot, -1),
                device_id_type=MESH,
            ).start()

    tables(0)
    load[0].wait()
    for copy in load[1:] + own:
        copy.start()
    payload(0, x_in.at[0], False, 0, xs, 0, BOTH, 0, HALF)
    pl.semaphore_wait(barrier, PEERS + 1)
    dispatch(0, 0, xs, 0, EARLY)
    payload(0, x_in.at[0], False, 0, xs, 0, BOTH, HALF, HALF)
    dispatch(0, 0, xs, 0, LATE)
    far = [
        to_partner(0, wg_ref.at[0, 0], wgu.at[:, pl.ds(0, FF)]),
        to_partner(1, wu_ref.at[0, 0], wgu.at[:, pl.ds(FF, FF)]),
        to_partner(2, wd_ref.at[0, 0], wd),
    ]
    load[1].wait()
    payload(0, dy_in, True, 1, ws, 0)
    dispatch(1, 1, ws, 0, OTHERS)
    for copy in far:
        copy.start()
    tables(1)
    load[2].wait()
    load[3].wait()
    payload(1, x_in.at[1], False, 2, xs, 2 * ALL)

    dispatch(4, 2, xs, 2 * ALL, EARLY)

    for copy in own:
        copy.wait()
    for copy in far:
        copy.wait()
    arrived(0)
    unfold(xs, 0, ALL)
    pair = [to_partner(3, xs.at[rows_of(0), :], xs.at[rows_of(1), :])]
    pair[-1].start()
    forward(0)
    arrived(1)
    dispatch(4, 2, xs, 2 * ALL, LATE)
    unfold(ws, 0, ALL)
    pair.append(to_partner(4, ws.at[rows_of(0), :], ws.at[rows_of(1), :]))
    pair[-1].start()
    for h in BOTH:
        hidden_part(0, 0, ALL, h)
    row_terms(0, 0, ALL)
    for h in BOTH:
        partials(0, 0, ALL, h, 2 + h)
    pair.append(to_partner(5, g_far.at[0], gs.at[rows_of(1), :]))
    pair[-1].start()
    pair.append(to_partner(6, h_far.at[0], hs.at[rows_of(1), :]))
    pair[-1].start()
    sent(0)

    relays = [
        pltpu.make_async_remote_copy(
            src_ref=first_ref.at[0, :, cols(h, 0, 8)], dst_ref=dy_next.at[:, cols(h, 0, 8)],
            send_sem=y_send.at[h], recv_sem=y_recv.at[h], device_id=before, device_id_type=MESH,
        )
        for h in BOTH
    ]

    def take(h):
        relays[h].wait()

        @pl.when(section == RING - 1)
        def _():
            dy_next[:, cols(h, 0, 8)] = last_in[:, cols(h, 0, 8)]

        payload(1, dy_next, True, 0, ws, 2 * ALL, (h,))

    arrived(2, OTHERS, (0,))
    combine(key.at[0], got, dy_in, first_ref.at[0], 0)
    relays[0].start()
    take(0)
    dispatch(5, 0, ws, 2 * ALL, OTHERS, (0,))
    arrived(3, OTHERS, (1,))
    combine(key.at[0], got, dy_in, first_ref.at[0], 1)
    relays[1].start()
    take(1)
    dispatch(6, 0, ws, 2 * ALL, OTHERS, (1,))

    sent(2, OTHERS, (0,))
    sent(3, OTHERS, (1,))
    arrived(5, OTHERS, (0,))
    unfold(ws, 2 * ALL, ALL, (0,))
    hidden_part(1, 0, ALL, 0)
    arrived(4)
    unfold(xs, 2 * ALL, ALL)
    pair.append(to_partner(7, xs.at[rows_of(2), :], xs.at[rows_of(3), :]))
    pair[-1].start()
    forward(1)
    arrived(6, OTHERS, (1,))
    unfold(ws, 2 * ALL, ALL, (1,))
    pair.append(to_partner(8, ws.at[rows_of(2), :], ws.at[rows_of(3), :]))
    pair[-1].start()
    hidden_part(1, 0, ALL, 1)
    row_terms(1, 0, ALL)
    pair.append(to_partner(9, g_far.at[1], gs.at[rows_of(3), :]))
    pair[-1].start()
    pair.append(to_partner(10, h_far.at[1], hs.at[rows_of(3), :]))
    pair[-1].start()
    for h in BOTH:
        partials(1, 0, ALL, h, 8 + h)

    for copy in pair:
        copy.wait()
    h_t[...] = hs[...].astype(F32).T.astype(BF16)

    def weight_body(d, carry):
        part = tile(d, 512)
        value = lax.dot_general(xs[:, part], gs[...], DOWN, preferred_element_type=F32)
        gg_ref[0, 0, part, :] = value[:, :FF].astype(BF16)
        gu_ref[0, 0, part, :] = value[:, FF:].astype(BF16)
        gd_ref[0, 0, :, part] = mm(h_t[...], ws[:, part]).astype(BF16)
        return carry

    lax.fori_loop(0, D // 512, weight_body, 0)

    for h in BOTH:
        arrived(8 + h, OTHERS, (h,))
    sent(1)
    sent(4)
    sent(5, OTHERS, (0,))
    sent(6, OTHERS, (1,))
    for h in BOTH:
        sent(8 + h, OTHERS, (h,))


def finish(
    first_ref, gg_ref, gu_ref, gd_ref, got, dy_next, key,
    first_out, second_out, gg_out, gu_out, gd_out, second, sem,
):
    copies = []

    def write(source, result):
        copies.append(pltpu.make_async_copy(source, result, sem.at[len(copies)]))
        copies[-1].start()

    for source, result in ((gg_ref, gg_out), (gu_ref, gu_out), (gd_ref, gd_out)):
        for p in range(4):
            rows = tile(p, source.shape[2] // 4)
            write(source.at[0, 0, rows, :], result.at[0, 0, rows, :])
    write(first_ref, first_out)
    for h in BOTH:
        combine(key.at[1], got, dy_next, second, h)
        write(second.at[:, cols(h, 0, 8)], second_out.at[0, :, cols(h, 0, 8)])
    for copy in copies:
        copy.wait()


def local(saved_inputs, arriving, last_grad, expert_ids, combine, w_gate, w_up, w_down):
    vmem = pl.BlockSpec(memory_space=pltpu.VMEM)
    hbm = pl.BlockSpec(memory_space=pl.ANY)
    dma = pltpu.SemaphoreType.DMA
    kept = [(a.shape, BF16) for a in (arriving, w_gate, w_up, w_down)]
    kept += [((ALL, 2 * WIDE), BF16), ((TOK, D), BF16), ((2, 2 * TOK, ALL), F32)]
    results = pl.pallas_call(
        kernel,
        out_shape=tuple(pltpu.VMEM(*k) for k in kept),
        in_specs=[hbm] * 3 + [vmem] * 2 + [hbm] * 3,
        out_specs=(vmem,) * 7,
        scratch_shapes=[
            pltpu.VMEM((2, TOK, D), BF16),
            pltpu.VMEM((TOK, D), BF16),
            pltpu.VMEM((TOK, D), BF16),
            pltpu.VMEM((D, 2 * FF), BF16),
            pltpu.VMEM((FF, D), BF16),
            pltpu.VMEM((4 * ALL, D), BF16),
            pltpu.VMEM((4 * ALL, D), BF16),
            pltpu.VMEM((4 * ALL, 2 * FF), BF16),
            pltpu.VMEM((4 * ALL, FF), BF16),
            pltpu.VMEM((2, ALL, 2 * FF), BF16),
            pltpu.VMEM((2, ALL, FF), BF16),
            pltpu.VMEM((3, ALL, 2 * WIDE), BF16),
            pltpu.VMEM((ALL, 2 * WIDE), BF16),
            pltpu.VMEM((2, ALL, 2 * FF), F32),
            pltpu.VMEM((ALL, 2 * FF), F32),
            pltpu.VMEM((2, ALL, 2 * TOK), F32),
            pltpu.VMEM((2, ALL, 2 * TOK), F32),
            pltpu.VMEM((FF, 4 * ALL), BF16),
            dma((10,)),
            dma((10,)),
            dma((4,)),
            dma((3,)),
            dma((11,)),
            dma((11,)),
            dma((2,)),
            dma((2,)),
        ],
        compiler_params=pltpu.CompilerParams(
            collective_id=0, has_side_effects=True, vmem_limit_bytes=50 << 20
        ),
        name="relay_backward",
    )(
        saved_inputs, arriving, last_grad, expert_ids.transpose(0, 3, 1, 2),
        combine.transpose(0, 3, 1, 2), w_gate, w_up, w_down,
    )
    return pl.pallas_call(
        finish,
        out_shape=tuple(
            jax.ShapeDtypeStruct(a.shape, BF16) for a in (arriving, arriving, w_gate, w_up, w_down)
        ),
        in_specs=[vmem] * 7,
        out_specs=(hbm,) * 5,
        scratch_shapes=[pltpu.VMEM((TOK, D), BF16), dma((15,))],
        compiler_params=pltpu.CompilerParams(vmem_limit_bytes=4 << 20),
        name="write_results",
    )(*[pltpu.with_memory_space_constraint(r, pltpu.VMEM) for r in results])


def solution(mesh):
    return jax.shard_map(
        local,
        mesh=mesh,
        in_specs=(
            P("section", None, "expert", None),
            P("section", "expert", None),
            P("expert", None),
            P("section", None, "expert", None),
            P("section", None, "expert", None),
            P("section", "expert", None, None),
            P("section", "expert", None, None),
            P("section", "expert", None, None),
        ),
        out_specs=(
            P("section", "expert", None),
            P("section", "expert", None),
            P("section", "expert", None, None),
            P("section", "expert", None, None),
            P("section", "expert", None, None),
        ),
        check_vma=False,
    )
```

```python
import jax
import jax.numpy as jnp
from jax import lax
from jax.experimental import pallas as pl
from jax.experimental.pallas import tpu as pltpu
from jax.sharding import PartitionSpec as P

MESH = pl.DeviceIdType.MESH
F32 = jnp.float32
BF16 = jnp.bfloat16

RING = 4
PEERS = RING * RING
ROWS = 16
CAP = 14
GROUP = 256
FULL = 7
WIDE = FULL * GROUP
D = 4096
SIDE = D // 2
BOTH = (0, 1)
TOK = 64
FF = 384
ALL = PEERS * ROWS

STEPS = (
    (0, 0), (2, 2), (1, 0), (-1, 2), (0, 1), (2, 1), (0, -1), (2, -1),
    (1, 2), (-1, 0), (1, 1), (0, 2), (-1, -1), (2, 0), (1, -1), (-1, 1),
)
EARLY, LATE, OTHERS = range(1, 8), range(8, 16), range(1, 16)
HALF = ALL // 2

ACROSS = (((1,), (1,)), ((), ()))
DOWN = (((0,), (0,)), ((), ()))


def mm(a, b):
    return jnp.dot(a, b, preferred_element_type=F32)


def mm_t(a, b):
    return lax.dot_general(a, b, ACROSS, preferred_element_type=F32)


def iota(shape, axis):
    return lax.broadcasted_iota(jnp.int32, shape, axis)


def spread(group, transposed, count):
    to, come = iota((count, count), int(transposed)), iota((count, count), int(not transposed))
    slot = to % ROWS
    late = (slot >= 7).astype(jnp.int32)
    hit = jnp.logical_and(come == to - slot + CAP + late, slot - 7 * late == group)
    return hit.astype(F32).astype(BF16)


def cols(half, group, count=1):
    return pl.ds(pl.multiple_of(half * SIDE + group * GROUP, GROUP), count * GROUP)


def sent_cols(half, group, count=1):
    return pl.ds(pl.multiple_of(half * WIDE + group * GROUP, GROUP), count * GROUP)


def tile(n, size):
    return pl.ds(pl.multiple_of(n * size, size), size)


def combine(table_of, got, grads, out, h, midway=None):
    total = jnp.zeros((TOK, GROUP), F32)
    for g in range(FULL):
        wanted = jnp.where(iota((2 * TOK, ALL), 0) < TOK, 0, g).astype(F32)
        table = jnp.where(table_of[...] == wanted, 1.0, 0.0).astype(BF16)
        value = mm(table, got[:, sent_cols(h, g)])
        out[:, cols(h, g)] = (grads[:, cols(h, g)].astype(F32) + value[:TOK]).astype(BF16)
        total = total + value[TOK:]
        if g == 3 and midway is not None:
            midway()
    tail = cols(h, FULL)
    out[:, tail] = (grads[:, tail].astype(F32) + total).astype(BF16)


def kernel(
    x_ref, dy_ref, last_ref, ids_ref, comb_ref, wg_ref, wu_ref, wd_ref,
    first_ref, gg_ref, gu_ref, gd_ref, got, dy_next, key,
    x_in, dy_in, last_in, wgu, wd, xs, ws, gs, hs, g_far, h_far, send, back,
    pre, hg, key_t, comb_t, h_t,
    ssem, rsem, isem, wsem, pair_send, pair_recv, y_send, y_recv,
):
    section = lax.axis_index("section")
    place = lax.axis_index("expert")
    at_x, at_z, core = place // (2 * RING), (place // 2) % RING, place % 2

    def expert_at(slot, sign):
        dx, dz = (sign * step % RING for step in STEPS[slot])
        return ((at_x + dx) % RING) * RING + (at_z + dz) % RING

    def chip(slot, sign):
        return (section, expert_at(slot, sign) * 2 + core)

    partner = (section, place + 1 - 2 * core)
    before = ((section + RING - 1) % RING, place)
    after = ((section + 1) % RING, place)

    barrier = pltpu.get_barrier_semaphore()
    for slot in range(1, PEERS):
        pl.semaphore_signal(barrier, inc=1, device_id=chip(slot, 1), device_id_type=MESH)
    pl.semaphore_signal(barrier, inc=1, device_id=partner, device_id_type=MESH)
    pl.semaphore_signal(barrier, inc=1, device_id=after, device_id_type=MESH)

    load = [
        pltpu.make_async_copy(x_ref.at[0, 0], x_in.at[0], isem.at[0]),
        pltpu.make_async_copy(dy_ref.at[0], dy_in, isem.at[1]),
        pltpu.make_async_copy(x_ref.at[0, 1], x_in.at[1], isem.at[2]),
        pltpu.make_async_copy(last_ref, last_in, isem.at[3]),
    ]
    load[0].start()

    own = [
        pltpu.make_async_copy(wg_ref.at[0, 0], gg_ref.at[0, 0], wsem.at[0]),
        pltpu.make_async_copy(wu_ref.at[0, 0], gu_ref.at[0, 0], wsem.at[1]),
        pltpu.make_async_copy(wd_ref.at[0, 0], gd_ref.at[0, 0], wsem.at[2]),
    ]

    def tables(m):
        shape = (ALL, 2 * TOK)
        row, lane = iota(shape, 0), iota(shape, 1)
        c = row % ROWS
        expert = jnp.concatenate(
            [jnp.full((ROWS, 2 * TOK), expert_at(slot, 1), jnp.int32) for slot in range(PEERS)], axis=0
        )
        named = jnp.zeros(shape, F32)
        combined = jnp.zeros(shape, F32)
        for k in range(3):
            ids = ids_ref[0, k, m : m + 1, :]
            weights = comb_ref[0, k, m : m + 1, :].astype(F32)
            hit = jnp.concatenate([ids, ids], axis=1) == expert
            named = jnp.where(hit, 1.0, named)
            combined = jnp.where(hit, jnp.concatenate([weights, weights], axis=1), combined)
        r2, c2 = iota((2 * TOK, 2 * TOK), 0), iota((2 * TOK, 2 * TOK), 1)
        earlier = (r2 < c2 % TOK).astype(F32).astype(BF16)
        rank = mm(named.astype(BF16), earlier)
        top = lane < TOK
        base = jnp.where(top, c, 7 * (c - CAP)).astype(F32)
        fits = jnp.logical_and(named > 0.5, top == (c < CAP))
        value = jnp.where(fits, rank - base, -100.0)
        key_t[m] = value
        key[m] = value.T
        comb_t[m] = combined

    def payload(m, source, scaled, buf, rows_ref, base, halves=BOTH, lo=0, count=ALL):
        def body(g, carry):
            data = jnp.concatenate(
                [
                    jnp.concatenate([source[:, cols(h, g)] for h in halves], axis=1),
                    jnp.concatenate([source[:, cols(h, FULL)] for h in halves], axis=1),
                ],
                axis=0,
            )
            lane = iota((count, 2 * TOK), 1)
            rows = pl.ds(lo, count)
            wanted = jnp.where(lane < TOK, 0, g).astype(F32)
            table = jnp.where(key_t[m, rows, :] == wanted, comb_t[m, rows, :] if scaled else 1.0, 0.0)
            value = mm(table.astype(BF16), data).astype(BF16)
            for n, h in enumerate(halves):
                piece = value[:, n * GROUP : (n + 1) * GROUP]
                send[buf, rows, sent_cols(h, g)] = piece
                if lo == 0:
                    rows_ref[pl.ds(base, ROWS), cols(h, g)] = piece[:ROWS]
            return carry

        lax.fori_loop(0, FULL, body, 0, unroll=True)

    def dispatch(phase, buf, rows_ref, base, slots, halves=BOTH):
        for slot in slots:
            for h in halves:
                pltpu.make_async_remote_copy(
                    src_ref=send.at[buf, pl.ds(slot * ROWS, ROWS), sent_cols(h, 0, FULL)],
                    dst_ref=rows_ref.at[pl.ds(base + slot * ROWS, ROWS), cols(h, 0, FULL)],
                    send_sem=ssem.at[phase],
                    recv_sem=rsem.at[phase],
                    device_id=chip(slot, 1),
                    device_id_type=MESH,
                ).start()

    def settle(sem, slots, halves):
        part = back.at[pl.ds(slots[0] * ROWS, len(slots) * ROWS), pl.ds(0, len(halves) * WIDE)]
        pltpu.make_async_copy(part, part, sem).wait()

    def sent(phase, slots=OTHERS, halves=BOTH):
        settle(ssem.at[phase], slots, halves)

    def arrived(phase, slots=OTHERS, halves=BOTH):
        settle(rsem.at[phase], slots, halves)

    def unfold(ref, base, count, halves=BOTH):
        total = jnp.zeros((count, len(halves) * GROUP), F32)
        rows = pl.ds(base, count)
        for g in range(FULL):
            block = jnp.concatenate([ref[rows, cols(h, g)] for h in halves], axis=1)
            total = total + mm(spread(g, False, count), block)
        for n, h in enumerate(halves):
            ref[rows, cols(h, FULL)] = total[:, n * GROUP : (n + 1) * GROUP].astype(BF16)

    def to_partner(n, src, dst):
        return pltpu.make_async_remote_copy(
            src_ref=src, dst_ref=dst, send_sem=pair_send.at[n], recv_sem=pair_recv.at[n],
            device_id=partner, device_id_type=MESH,
        )

    def rows_of(part):
        return pl.ds(part * ALL, ALL)

    def forward(m):
        base = 2 * m * ALL

        def body(n, carry):
            pre[1, :, tile(n, 256)] = mm(xs[pl.ds(base, ALL), :], wgu[:, tile(n, 256)])
            return carry

        for n in range(3):
            lo, hi = n * 256, (n + 1) * 256
            pieces = [gg_ref[0, 0, :, lo : min(hi, FF)]] if lo < FF else []
            if hi > FF:
                pieces.append(gu_ref[0, 0, :, max(lo - FF, 0) : hi - FF])
            block = pieces[0] if len(pieces) == 1 else jnp.concatenate(pieces, axis=1)
            pre[0, :, lo:hi] = mm(xs[pl.ds(base, ALL), :], block)
        lax.fori_loop(0, 3, body, 0)

    def hidden_part(m, lo, count, h):
        rows, part = pl.ds(2 * m * ALL + lo, count), cols(h, 0, 8)

        for half, weights in ((0, gd_ref.at[0, 0]), (1, wd)):
            value = mm_t(weights[:, part], ws[rows, part]).T
            if h:
                value = value + hg[pl.ds(lo, count), half * FF : (half + 1) * FF]
            hg[pl.ds(lo, count), half * FF : (half + 1) * FF] = value

    def row_terms(m, lo, count):
        base = 2 * m * ALL + lo
        real = iota((count, FF), 0) % ROWS < CAP
        part = pl.ds(lo, count)
        for half in range(2):
            gate, up = pre[half, part, :FF], pre[half, part, FF:]
            grad = hg[part, half * FF : (half + 1) * FF]
            sig = jax.nn.sigmoid(gate)
            active = gate * sig
            hidden = jnp.where(real, active * up, 0.0).astype(BF16)
            gate_rows = grad * up * sig * (1.0 + gate * (1.0 - sig))
            gate_rows = jnp.where(real, gate_rows, 0.0).astype(BF16)
            up_rows = jnp.where(real, grad * active, 0.0).astype(BF16)
            if half == 0:
                gs[pl.ds(base, count), :FF] = gate_rows
                gs[pl.ds(base, count), FF:] = up_rows
                hs[pl.ds(base, count), :] = hidden
            else:
                g_far[m, part, :FF] = gate_rows
                g_far[m, part, FF:] = up_rows
                h_far[m, part, :] = hidden

    def partials(m, lo, count, h, phase):
        def pair_of(n):
            part = cols(h, 2 * n, 2)
            own_part = jnp.concatenate([gg_ref[0, 0, part, :], gu_ref[0, 0, part, :]], axis=1)
            near = mm_t(gs[pl.ds(2 * m * ALL + lo, count), :], own_part)
            return near + mm_t(g_far[m, pl.ds(lo, count), :], wgu[part, :])

        def keep(g, value):
            value = (value + mm(spread(g, True, count), folded)).astype(BF16)
            back[pl.ds(lo, count), sent_cols(h, g)] = value
            if lo == 0:
                got[pl.ds(0, ROWS), sent_cols(h, g)] = value[:ROWS]

        last = pair_of(3)
        folded = last[:, GROUP:].astype(BF16)
        keep(6, last[:, :GROUP])

        def both(n):
            value = pair_of(n)
            keep(2 * n, value[:, :GROUP])
            keep(2 * n + 1, value[:, GROUP:])

        both(2)
        give_back(phase, h, 4, 3)
        both(1)
        both(0)
        give_back(phase, h, 0, 4)

    def give_back(phase, h, group, count):
        for slot in OTHERS:
            pltpu.make_async_remote_copy(
                src_ref=back.at[pl.ds(slot * ROWS, ROWS), sent_cols(h, group, count)],
                dst_ref=got.at[pl.ds(slot * ROWS, ROWS), sent_cols(h, group, count)],
                send_sem=ssem.at[phase],
                recv_sem=rsem.at[phase],
                device_id=chip(slot, -1),
                device_id_type=MESH,
            ).start()

    tables(0)
    load[0].wait()
    for copy in load[1:] + own:
        copy.start()
    payload(0, x_in.at[0], False, 0, xs, 0, BOTH, 0, HALF)
    pl.semaphore_wait(barrier, PEERS + 1)
    dispatch(0, 0, xs, 0, EARLY)
    payload(0, x_in.at[0], False, 0, xs, 0, BOTH, HALF, HALF)
    dispatch(0, 0, xs, 0, LATE)
    far = [
        to_partner(0, wg_ref.at[0, 0], wgu.at[:, pl.ds(0, FF)]),
        to_partner(1, wu_ref.at[0, 0], wgu.at[:, pl.ds(FF, FF)]),
        to_partner(2, wd_ref.at[0, 0], wd),
    ]
    load[1].wait()
    payload(0, dy_in, True, 1, ws, 0)
    dispatch(1, 1, ws, 0, OTHERS)
    for copy in far:
        copy.start()
    tables(1)
    load[2].wait()
    load[3].wait()
    payload(1, x_in.at[1], False, 2, xs, 2 * ALL)

    dispatch(4, 2, xs, 2 * ALL, EARLY)

    for copy in own:
        copy.wait()
    for copy in far:
        copy.wait()
    arrived(0)
    unfold(xs, 0, ALL)
    pair = [to_partner(3, xs.at[rows_of(0), :], xs.at[rows_of(1), :])]
    pair[-1].start()
    forward(0)
    arrived(1)
    dispatch(4, 2, xs, 2 * ALL, LATE)
    unfold(ws, 0, ALL)
    pair.append(to_partner(4, ws.at[rows_of(0), :], ws.at[rows_of(1), :]))
    pair[-1].start()
    for h in BOTH:
        hidden_part(0, 0, ALL, h)
    row_terms(0, 0, ALL)
    for h in BOTH:
        partials(0, 0, ALL, h, 2 + h)
    pair.append(to_partner(5, g_far.at[0], gs.at[rows_of(1), :]))
    pair[-1].start()
    pair.append(to_partner(6, h_far.at[0], hs.at[rows_of(1), :]))
    pair[-1].start()
    sent(0)

    relays = [
        pltpu.make_async_remote_copy(
            src_ref=first_ref.at[0, :, cols(q // 2, q % 2 * 4, 4)],
            dst_ref=dy_next.at[:, cols(q // 2, q % 2 * 4, 4)],
            send_sem=y_send.at[q], recv_sem=y_recv.at[q], device_id=before, device_id_type=MESH,
        )
        for q in range(4)
    ]

    def take(h):
        relays[2 * h].wait()
        relays[2 * h + 1].wait()

        @pl.when(section == RING - 1)
        def _():
            dy_next[:, cols(h, 0, 8)] = last_in[:, cols(h, 0, 8)]

        payload(1, dy_next, True, 0, ws, 2 * ALL, (h,))

    arrived(2, OTHERS, (0,))
    combine(key.at[0], got, dy_in, first_ref.at[0], 0, relays[0].start)
    relays[1].start()
    take(0)
    dispatch(5, 0, ws, 2 * ALL, OTHERS, (0,))
    arrived(3, OTHERS, (1,))
    combine(key.at[0], got, dy_in, first_ref.at[0], 1, relays[2].start)
    relays[3].start()
    take(1)
    dispatch(6, 0, ws, 2 * ALL, OTHERS, (1,))

    sent(2, OTHERS, (0,))
    sent(3, OTHERS, (1,))
    arrived(5, OTHERS, (0,))
    unfold(ws, 2 * ALL, ALL, (0,))
    hidden_part(1, 0, ALL, 0)
    arrived(4)
    unfold(xs, 2 * ALL, ALL)
    pair.append(to_partner(7, xs.at[rows_of(2), :], xs.at[rows_of(3), :]))
    pair[-1].start()
    forward(1)
    arrived(6, OTHERS, (1,))
    unfold(ws, 2 * ALL, ALL, (1,))
    pair.append(to_partner(8, ws.at[rows_of(2), :], ws.at[rows_of(3), :]))
    pair[-1].start()
    hidden_part(1, 0, ALL, 1)
    row_terms(1, 0, ALL)
    pair.append(to_partner(9, g_far.at[1], gs.at[rows_of(3), :]))
    pair[-1].start()
    pair.append(to_partner(10, h_far.at[1], hs.at[rows_of(3), :]))
    pair[-1].start()
    for h in BOTH:
        partials(1, 0, ALL, h, 8 + h)

    for copy in pair:
        copy.wait()
    h_t[...] = hs[...].astype(F32).T.astype(BF16)

    def weight_body(d, carry):
        part = tile(d, 512)
        value = lax.dot_general(xs[:, part], gs[...], DOWN, preferred_element_type=F32)
        gg_ref[0, 0, part, :] = value[:, :FF].astype(BF16)
        gu_ref[0, 0, part, :] = value[:, FF:].astype(BF16)
        gd_ref[0, 0, :, part] = mm(h_t[...], ws[:, part]).astype(BF16)
        return carry

    lax.fori_loop(0, D // 512, weight_body, 0)

    for h in BOTH:
        arrived(8 + h, OTHERS, (h,))
    sent(1)
    sent(4)
    sent(5, OTHERS, (0,))
    sent(6, OTHERS, (1,))
    for h in BOTH:
        sent(8 + h, OTHERS, (h,))


def finish(
    first_ref, gg_ref, gu_ref, gd_ref, got, dy_next, key,
    first_out, second_out, gg_out, gu_out, gd_out, second, sem,
):
    copies = []

    def write(source, result):
        copies.append(pltpu.make_async_copy(source, result, sem.at[len(copies)]))
        copies[-1].start()

    for source, result in ((gg_ref, gg_out), (gu_ref, gu_out), (gd_ref, gd_out)):
        for p in range(4):
            rows = tile(p, source.shape[2] // 4)
            write(source.at[0, 0, rows, :], result.at[0, 0, rows, :])
    write(first_ref, first_out)
    for h in BOTH:
        combine(key.at[1], got, dy_next, second, h)
        write(second.at[:, cols(h, 0, 8)], second_out.at[0, :, cols(h, 0, 8)])
    for copy in copies:
        copy.wait()


def local(saved_inputs, arriving, last_grad, expert_ids, combine, w_gate, w_up, w_down):
    vmem = pl.BlockSpec(memory_space=pltpu.VMEM)
    hbm = pl.BlockSpec(memory_space=pl.ANY)
    dma = pltpu.SemaphoreType.DMA
    kept = [(a.shape, BF16) for a in (arriving, w_gate, w_up, w_down)]
    kept += [((ALL, 2 * WIDE), BF16), ((TOK, D), BF16), ((2, 2 * TOK, ALL), F32)]
    results = pl.pallas_call(
        kernel,
        out_shape=tuple(pltpu.VMEM(*k) for k in kept),
        in_specs=[hbm] * 3 + [vmem] * 2 + [hbm] * 3,
        out_specs=(vmem,) * 7,
        scratch_shapes=[
            pltpu.VMEM((2, TOK, D), BF16),
            pltpu.VMEM((TOK, D), BF16),
            pltpu.VMEM((TOK, D), BF16),
            pltpu.VMEM((D, 2 * FF), BF16),
            pltpu.VMEM((FF, D), BF16),
            pltpu.VMEM((4 * ALL, D), BF16),
            pltpu.VMEM((4 * ALL, D), BF16),
            pltpu.VMEM((4 * ALL, 2 * FF), BF16),
            pltpu.VMEM((4 * ALL, FF), BF16),
            pltpu.VMEM((2, ALL, 2 * FF), BF16),
            pltpu.VMEM((2, ALL, FF), BF16),
            pltpu.VMEM((3, ALL, 2 * WIDE), BF16),
            pltpu.VMEM((ALL, 2 * WIDE), BF16),
            pltpu.VMEM((2, ALL, 2 * FF), F32),
            pltpu.VMEM((ALL, 2 * FF), F32),
            pltpu.VMEM((2, ALL, 2 * TOK), F32),
            pltpu.VMEM((2, ALL, 2 * TOK), F32),
            pltpu.VMEM((FF, 4 * ALL), BF16),
            dma((10,)),
            dma((10,)),
            dma((4,)),
            dma((3,)),
            dma((11,)),
            dma((11,)),
            dma((4,)),
            dma((4,)),
        ],
        compiler_params=pltpu.CompilerParams(
            collective_id=0, has_side_effects=True, vmem_limit_bytes=50 << 20
        ),
        name="relay_backward",
    )(
        saved_inputs, arriving, last_grad, expert_ids.transpose(0, 3, 1, 2),
        combine.transpose(0, 3, 1, 2), w_gate, w_up, w_down,
    )
    return pl.pallas_call(
        finish,
        out_shape=tuple(
            jax.ShapeDtypeStruct(a.shape, BF16) for a in (arriving, arriving, w_gate, w_up, w_down)
        ),
        in_specs=[vmem] * 7,
        out_specs=(hbm,) * 5,
        scratch_shapes=[pltpu.VMEM((TOK, D), BF16), dma((15,))],
        compiler_params=pltpu.CompilerParams(vmem_limit_bytes=4 << 20),
        name="write_results",
    )(*[pltpu.with_memory_space_constraint(r, pltpu.VMEM) for r in results])


def solution(mesh):
    return jax.shard_map(
        local,
        mesh=mesh,
        in_specs=(
            P("section", None, "expert", None),
            P("section", "expert", None),
            P("expert", None),
            P("section", None, "expert", None),
            P("section", None, "expert", None),
            P("section", "expert", None, None),
            P("section", "expert", None, None),
            P("section", "expert", None, None),
        ),
        out_specs=(
            P("section", "expert", None),
            P("section", "expert", None),
            P("section", "expert", None, None),
            P("section", "expert", None, None),
            P("section", "expert", None, None),
        ),
        check_vma=False,
    )
```
